256 devices in a mesh: sx: 16 (over z, core), sy: 16 (over x, y).
Axes of the slice: x: 4, y: 4, z: 8, core: 2. Of those that a mesh axis runs over, the one named last changes fastest.
Arguments:
- factor_inv: bfloat16 [32, 16, 1024, 1024], P('sx', 'sy'), as said below
- dirichlet: bfloat16 [32, 16, 1024, 1024], P('sx', 'sy')
- coarse_inv: bfloat16 [4096, 4096], P('sy'), as said below
- domain_sizes: int32 [32, 16], P('sx', 'sy'), may hold values from 32 to 256, as said below
- corner_map: int32 [32, 16, 32], P('sx', 'sy'), may hold values from 0 to 4095
- snow_level: int32 [32, 16, 1024], P('sx', 'sy'), may hold values from 0 to 7
- pressure: bfloat16 [32, 16, 1024, 128], P('sx', 'sy'), may hold values from -6 to 6
Outputs:
- multiplier: float32 [32, 16, 1024, 128], P('sx', 'sy')
- residual: float32 [32, 16, 1024, 128], P('sx', 'sy')
The draws below stay inside these ranges and needn't reach their ends.
Inputs may be any that keep to these rules, and one draw needn't show every extreme that they name: `domain_sizes`: each edge's active unknowns are its first ones; some subdomain has all 256. `factor_inv`: lower triangular. `coarse_inv`: Symmetric.
All inputs are finite; a program needn't handle non-finite values.
Results may differ from the reference program's by a relative error of at most 0.0034.
Values may be sent and summed in bfloat16 or wider, within the bound.
No kernel may reach another device: no remote copies, remote signals or barrier semaphores. Data moves between devices by JAX's collectives and lax.ppermute only.
A program may use at most 128 MiB of HBM per device.

```python
import math
import jax
import jax.numpy as jnp
from jax import lax

B = 1024
E = 256
K = 128
CORN = 32
NC = 4096
ITERS = 2
GR = 32
GC = 16


def draw_factor_inv(key, part):
    key_diag, key_off = jax.random.split(jax.random.fold_in(key, 11))
    diagonal = jax.random.uniform(key_diag, (GR, GC, B), jnp.float32, 1.0, 2.0)
    spread_off = jax.random.normal(key_off, (GR, GC, B, B), jnp.float32)
    position = jnp.arange(B)
    below_diag = position[:, None] > position[None, :]
    diagonal_pos = position[:, None] == position[None, :]
    scaled = spread_off * (0.7 / math.sqrt(B))
    result = jnp.where(diagonal_pos, diagonal[..., None], jnp.where(below_diag, scaled, 0.0))
    return result.astype(jnp.bfloat16)


def draw_dirichlet(key, part):
    key_diag, key_off = jax.random.split(jax.random.fold_in(key, 23))
    diagonal = jax.random.uniform(key_diag, (GR, GC, B), jnp.float32, 1.0, 2.0)
    spread_off = jax.random.normal(key_off, (GR, GC, B, B), jnp.float32)
    position = jnp.arange(B)
    diagonal_pos = position[:, None] == position[None, :]
    scaled = spread_off * (0.5 / math.sqrt(B))
    result = jnp.where(diagonal_pos, diagonal[..., None], scaled)
    return result.astype(jnp.bfloat16)


def draw_coarse_inv(key, part):
    key_diag, key_off = jax.random.split(jax.random.fold_in(key, 37))
    diagonal = jax.random.uniform(key_diag, (NC,), jnp.float32, 1.0, 2.0)
    noise = jax.random.normal(key_off, (NC, NC), jnp.float32)
    symmetric = (noise + noise.T) * (0.35 / math.sqrt(NC))
    position = jnp.arange(NC)
    diagonal_pos = position[:, None] == position[None, :]
    result = jnp.where(diagonal_pos, diagonal[:, None], symmetric)
    return result.astype(jnp.bfloat16)


def draw_domain_sizes(key, part):
    key_light, key_heavy, key_pick, key_spot = jax.random.split(jax.random.fold_in(key, 41), 4)
    light_size = jax.random.randint(key_light, (GR, GC), E // 8, E // 2 + 1)
    heavy_size = jax.random.randint(key_heavy, (GR, GC), E // 2 + 1, E + 1)
    chosen = jax.random.randint(key_pick, (GR, GC), 0, 32) == 0
    values = jnp.where(chosen, heavy_size, light_size).reshape(-1)
    target = jax.random.randint(key_spot, (), 0, GR * GC)
    flat_index = jnp.arange(GR * GC)
    values = jnp.where(flat_index == target, E, values)
    return values.reshape(GR, GC).astype(jnp.int32)


def with_ends(values, rng, low, top_value):
    index_at = [jax.random.randint(jax.random.fold_in(rng, axis), (), 0, length) for axis, length in enumerate(values.shape)]
    widest = values.shape.index(max(values.shape))
    beside = index_at[:widest] + [(index_at[widest] + 1) % values.shape[widest]] + index_at[widest + 1:]
    return values.at[tuple(index_at)].set(low).at[tuple(beside)].set(top_value)


def shard_levels(key, dims, cuts, least, high):
    factor_of, own = 1.0, jax.random.fold_in(key, 6)
    for dim, parts in cuts:
        heights = jnp.exp(jax.random.uniform(jax.random.fold_in(own, dim), (parts,), jnp.float32, least / len(cuts), high / len(cuts)))
        factor_of = factor_of * jnp.repeat(heights, dims[dim] // parts).reshape([-1 if axis == dim else 1 for axis in range(len(dims))])
    return factor_of


def normal_values(own_key, shape, width, bound, cuts=(), kind=jnp.bfloat16):
    gain = shard_levels(own_key, shape, cuts, -0.22, 0.18) if cuts else 1.0
    values = jax.random.normal(own_key, shape, jnp.float32) * width * gain
    return jnp.minimum(jnp.maximum(values, -bound), bound).astype(kind)


def setup_inputs(seed: int = 0) -> dict:
    keys = jax.random.split(jax.random.key(seed), 8)
    factor_inv = draw_factor_inv(jax.random.fold_in(keys[7], 71), 0)
    dirichlet = draw_dirichlet(jax.random.fold_in(keys[7], 71), 0)
    coarse_inv = draw_coarse_inv(jax.random.fold_in(keys[7], 71), 0)
    domain_sizes = draw_domain_sizes(jax.random.fold_in(keys[7], 71), 0)
    corner_map = with_ends(jax.random.randint(keys[4], (GR, GC, CORN), 0, NC), jax.random.fold_in(keys[4], 1), 0, NC - 1).astype(jnp.int32)
    snow_level = with_ends(jax.random.randint(keys[5], (GR, GC, B), 0, 8), jax.random.fold_in(keys[5], 1), 0, 7).astype(jnp.int32)
    pressure = normal_values(keys[6], (GR, GC, B, K), 1.0, 6.0, ((0, 16), (1, 16)))
    return dict(factor_inv=factor_inv, dirichlet=dirichlet, coarse_inv=coarse_inv, domain_sizes=domain_sizes, corner_map=corner_map, snow_level=snow_level, pressure=pressure)


def active_mask(domain_sizes):
    offsets = jnp.arange(B, dtype=jnp.int32) % E
    return (offsets[None, None, :] < domain_sizes[:, :, None]).astype(jnp.float32)[..., None]


def per_domain(matrices, vectors, transpose):
    stacked_mat = matrices.reshape((GR * GC,) + matrices.shape[2:])
    stacked_vec = vectors.reshape((GR * GC,) + vectors.shape[2:])

    def single(operands):
        matrix, vector = operands
        if transpose:
            return lax.dot_general(matrix, vector, (((0,), (0,)), ((), ())), preferred_element_type=jnp.float32)
        return jnp.dot(matrix, vector, preferred_element_type=jnp.float32)

    result = lax.map(single, (stacked_mat, stacked_vec))
    return result.reshape((GR, GC) + result.shape[1:])


def jump(interface):
    north_edge = interface[:, :, 0:E]
    south_edge = interface[:, :, E:2 * E]
    west_edge = interface[:, :, 2 * E:3 * E]
    east_edge = interface[:, :, 3 * E:4 * E]
    from_above = jnp.concatenate([jnp.zeros_like(south_edge[:1]), south_edge[:-1]], axis=0)
    from_below = jnp.concatenate([north_edge[1:], jnp.zeros_like(north_edge[:1])], axis=0)
    from_left = jnp.concatenate([jnp.zeros_like(east_edge[:, :1]), east_edge[:, :-1]], axis=1)
    from_right = jnp.concatenate([west_edge[:, 1:], jnp.zeros_like(west_edge[:, :1])], axis=1)
    return jnp.concatenate([north_edge - from_above, south_edge - from_below, west_edge - from_left, east_edge - from_right], axis=2)


def reference(factor_inv, dirichlet, coarse_inv, domain_sizes, corner_map, snow_level, pressure):
    active = active_mask(domain_sizes)
    grid_row = jnp.arange(GR, dtype=jnp.float32)[:, None]
    grid_col = jnp.arange(GC, dtype=jnp.float32)[None, :]
    drift_factor = 1.0 + 2.0 * (grid_row + grid_col) / (GR + GC - 2)
    depth = 0.5 + 0.25 * snow_level.astype(jnp.float32)
    loading = pressure.astype(jnp.float32) * depth[..., None] * drift_factor[:, :, None, None] * active
    stride = B // CORN
    factor_corner = factor_inv[:, :, :, ::stride]
    multiplier = jnp.zeros_like(loading)
    residual = loading
    for iteration in range(ITERS):
        search = active * per_domain(dirichlet, residual.astype(jnp.bfloat16), False)
        inner_term = per_domain(factor_inv, search.astype(jnp.bfloat16), False).astype(jnp.bfloat16)
        interface = active * per_domain(factor_inv, inner_term, True)
        corners = interface[:, :, ::stride]
        coarse_res = jnp.zeros((NC, K), jnp.float32).at[corner_map.reshape(-1)].add(corners.reshape(-1, K))
        coarse_sol = jnp.dot(coarse_inv, coarse_res.astype(jnp.bfloat16), preferred_element_type=jnp.float32).astype(jnp.bfloat16)
        picked = coarse_sol[corner_map]
        lifted = per_domain(factor_corner, picked, False).astype(jnp.bfloat16)
        interface = active * (interface + per_domain(factor_inv, lifted, True))
        jumped = active * jump(interface)
        cross_term = jnp.sum(residual * jumped, axis=(0, 1, 2))
        energy = jnp.sum(jumped * jumped, axis=(0, 1, 2))
        step_size = cross_term / (energy + 1e-6)
        multiplier = multiplier + step_size * search
        residual = residual - step_size * jumped
    return multiplier, residual
```

```python
import jax
import jax.numpy as jnp
from jax import lax
from jax.experimental import pallas as pl
from jax.experimental.pallas import tpu as pltpu
from jax.sharding import Mesh
from jax.sharding import PartitionSpec as P

B = 1024
E = 256
K = 128
CORN = 32
NC = 4096
GR = 32
GC = 16
ZS = 8
CS = 2
XS = 4
YS = 4
SY = XS * YS
STRIDE = B // CORN
ROWS = 80
HALF = 128
F32 = jnp.float32
BF16 = jnp.bfloat16
VMEM_LIMIT = 48 * 1024 * 1024

VM = pl.BlockSpec(memory_space=pltpu.VMEM)
SM = pl.BlockSpec(memory_space=pltpu.SMEM)
HB = pl.BlockSpec(memory_space=pl.ANY)


def dot(a, b):
    return jnp.dot(a, b, preferred_element_type=F32)


def iota(shape, dim):
    return lax.broadcasted_iota(jnp.int32, shape, dim)


def call(kernel, outs, in_specs, scratch=()):
    return pl.pallas_call(
        kernel,
        out_shape=[jax.ShapeDtypeStruct(shape, dtype) for shape, dtype in outs],
        in_specs=in_specs,
        out_specs=[VM] * len(outs),
        scratch_shapes=list(scratch),
        compiler_params=pltpu.CompilerParams(vmem_limit_bytes=VMEM_LIMIT),
    )


def split2(value):
    high = value.astype(BF16)
    low = (value - high.astype(F32)).astype(BF16)
    return high, low


def split3(value):
    high, _ = split2(value)
    rest = value - high.astype(F32)
    mid, low = split2(rest)
    return high, mid, low


def active_mask(size):
    return ((iota((B, K), 0) & (E - 1)) < size).astype(F32)


def rows_of(shape, rows):
    index = iota(shape, 0)
    result = jnp.zeros(shape, F32)
    for number, row in enumerate(rows):
        result = jnp.where(index == number, jnp.broadcast_to(row.astype(F32), shape), result)
    return result


def write_payload(pay, interface, tail):
    corners = [interface[s, pl.ds(0, CORN, stride=STRIDE), :].astype(BF16) for s in range(2)]
    block = jnp.concatenate(corners + [tail.astype(BF16)], axis=0)
    for dest in range(SY):
        pay[dest] = block


def write_edges(refs, interface, extra):
    north, south, west, east = refs

    def packed(s, edge):
        rows = pl.ds(edge * E, E)
        parts = list(split2(interface[s, rows, :]))
        if extra is not None:
            parts.append(extra[s, rows, :])
        return jnp.concatenate(parts, axis=1)

    north[...] = packed(0, 0)
    south[...] = packed(1, 1)
    for s in range(2):
        west[s] = packed(s, 2)
        east[s] = packed(s, 3)


def first_kernel(sizes, snow, cmap, press, dir_hbm, fac_hbm,
                 res, search, inter, gram, pay, north, south, west, east,
                 dbuf, lbuf, sems):
    copies = []
    for s in range(2):
        copies.append(pltpu.make_async_copy(dir_hbm.at[s], dbuf.at[s], sems.at[s]))
        copies.append(pltpu.make_async_copy(fac_hbm.at[s], lbuf.at[s], sems.at[2 + s]))
    copies[0].start()
    copies[2].start()
    copies[1].start()
    copies[3].start()
    grid_row = lax.axis_index("z") * (2 * CS) + lax.axis_index("core") * 2
    grid_col = lax.axis_index("x") * YS + lax.axis_index("y")
    lane = iota((B, K), 1)
    masks = [active_mask(sizes[s]) for s in range(2)]
    pick_col = jnp.where((iota((B, K), 0) == lane * STRIDE) & (lane < CORN), 1.0, 0.0).astype(BF16)
    for s in range(2):
        place = jnp.full((K, B), grid_row + s + grid_col, jnp.int32).astype(F32)
        drift = 1.0 + 2.0 * place / (GR + GC - 2)
        depth = 0.5 + 0.25 * jnp.broadcast_to(snow[s : s + 1, :], (K, B)).astype(F32)
        res[s] = press[s].astype(F32) * jnp.transpose(depth) * jnp.transpose(drift) * masks[s]
    cm = cmap[...]
    for s in range(2):
        copies[2 * s].wait()
        found = masks[s] * dot(dbuf[s], res[s].astype(BF16))
        search[s] = found
    for s in range(2):
        copies[2 * s + 1].wait()
        right = jnp.concatenate([search[s].astype(BF16), pick_col], axis=1)
        inner = jnp.transpose(dot(lbuf[s], right)).astype(BF16)
        back = jnp.transpose(dot(inner, lbuf[s]))
        inter[s] = masks[s] * back[:, :K]
        ghigh, glow = split2(masks[s] * back[:, K:])
        square = jnp.transpose(jnp.broadcast_to(cm[s : s + 1, :], (K, K)))
        column = jnp.concatenate([square] * (B // K), axis=0)
        digits = jnp.where(lane < 96, column >> 8, column & 255).astype(F32)
        low_moved = pltpu.roll(glow.astype(F32), CORN, axis=1)
        gram[s] = jnp.where(
            lane < CORN, ghigh.astype(F32), jnp.where(lane < 2 * CORN, low_moved, digits)
        ).astype(BF16)
    both = cm[2:3, :]
    tail = rows_of((16, K), [(both >> 8).astype(F32), (both & 255).astype(F32)])
    write_payload(pay, inter, tail)
    write_edges((north, south, west, east), inter, gram)


def coarse_rows(rec):
    return jnp.concatenate([rec[b, 0:64, :] for b in range(SY)], axis=0)


def halves(value, stats, own, snd):
    mine = lax.axis_index("core") == 0
    tail = rows_of((8, K), stats)
    own[0:HALF] = jnp.where(mine, value[:HALF], value[HALF:])
    snd[0:HALF] = jnp.where(mine, value[HALF:], value[:HALF])
    own[HALF : HALF + 8] = tail
    snd[HALF : HALF + 8] = tail


def coarse_first_kernel(rec, coarse, own, snd, picked_inv, acc):
    lane = iota((1, K), 1)
    tails = [rec[b, 64:80, :].astype(F32) for b in range(SY)]

    def row(number):
        parts = [
            jnp.where(lane < 64, tails[2 * m][number : number + 1], tails[2 * m + 1][number : number + 1])
            for m in range(SY // 2)
        ]
        return jnp.concatenate(parts, axis=1)

    high, low = row(0), row(1)
    low_hot = jnp.where(iota((E, B), 0) == low.astype(jnp.int32), 1.0, 0.0).astype(BF16)
    for digit in range(NC // E):
        part = dot(coarse[:, digit * E : (digit + 1) * E], low_hot)
        part = jnp.where(high == digit, part, 0.0)
        if digit == 0:
            acc[...] = part
        else:
            acc[...] += part
    matrix = acc[...].astype(BF16)
    picked_inv[...] = matrix
    halves(dot(matrix, coarse_rows(rec)), [], own, snd)


def coarse_next_kernel(rec, picked_inv, own, snd):
    value = dot(picked_inv[...], coarse_rows(rec))
    tails = sum(rec[b, 64:80, :].astype(F32) for b in range(SY))
    stats = [tails[q : q + 1] + tails[q + 1 : q + 2] + tails[q + 2 : q + 3] for q in (2, 5)]
    halves(value, stats, own, snd)


def pair_sum_kernel(own, rcv, pay):
    total = own[...] + rcv[...]
    rows = []
    for q in range(2):
        rows += list(split3(total[HALF + q : HALF + q + 1]))
    tail = rows_of((16, K), rows).astype(BF16)
    block = jnp.concatenate([total[:HALF].astype(BF16), tail], axis=0)
    for dest in range(ZS):
        pay[dest] = block


def z_sum_kernel(rec, pay, stats):
    total = sum(rec[z].astype(F32) for z in range(ZS))
    block = total[:HALF].astype(BF16)
    for dest in range(SY):
        pay[dest] = block
    rows = total[HALF:]
    stats[...] = rows_of(
        (8, K), [rows[q : q + 1] + rows[q + 1 : q + 2] + rows[q + 2 : q + 3] for q in (0, 3)]
    )


def jumps(sizes, sol_own, sol_other, inter, gram, edges, grams):
    core = lax.axis_index("core")
    in_north, in_south, in_west, in_east = edges
    gram_edges = [gram[0, 0:CORN, :], gram[1, 0:CORN, :]]
    gram_edges += [g[0:CORN, :] for g in grams[:2]]
    gram_edges += [g[s, 0:CORN, :] for g in grams[2:] for s in range(2)]
    digits = jnp.concatenate(gram_edges, axis=0).astype(F32)
    cm = digits[:, 64:65].astype(jnp.int32) * 256 + digits[:, 96:97].astype(jnp.int32)
    half = ((cm >> 7) & 1) ^ core
    place = half * 2048 + (cm >> 8) * HALF + (cm & (HALF - 1))
    hot = jnp.where(iota((8 * CORN, NC), 1) == place, 1.0, 0.0).astype(BF16)
    picks = (dot(hot[:, :2048], sol_own[...]) + dot(hot[:, 2048:], sol_other[...])).astype(BF16)
    zero = jnp.zeros((2 * CORN, K), BF16)

    def stacked(number):
        rows = picks[number * CORN : (number + 1) * CORN]
        return jnp.concatenate([rows, rows, zero], axis=0)

    full = [inter[s] + dot(gram[s], stacked(s)) for s in range(2)]

    def arrived(edge, gedge, number):
        return edge[:, :K].astype(F32) + edge[:, K : 2 * K].astype(F32) + dot(gedge, stacked(number))

    above = [arrived(in_north[...], grams[0], 2), full[0][E : 2 * E]]
    below = [full[1][0:E], arrived(in_south[...], grams[1], 3)]
    left = [arrived(in_west[s], grams[2][s], 4 + s) for s in range(2)]
    right = [arrived(in_east[s], grams[3][s], 6 + s) for s in range(2)]
    return [
        active_mask(sizes[s]) * (full[s] - jnp.concatenate([above[s], below[s], left[s], right[s]], axis=0))
        for s in range(2)
    ]


def second_kernel(sizes, sol_own, sol_other, inter, gram, in_north, in_south, in_west, in_east,
                  res, dir_hbm, fac_hbm,
                  jump0, prod, inter1, pay, north, south, west, east,
                  dbuf, lbuf, sems):
    copies = []
    for s in range(2):
        copies.append(pltpu.make_async_copy(dir_hbm.at[s], dbuf.at[s], sems.at[s]))
        copies.append(pltpu.make_async_copy(fac_hbm.at[s], lbuf.at[s], sems.at[2 + s]))
    copies[0].start()
    copies[2].start()
    copies[1].start()
    copies[3].start()
    grams = [in_north[:, 2 * K :], in_south[:, 2 * K :], in_west[:, :, 2 * K :], in_east[:, :, 2 * K :]]
    jumped = jumps(sizes, sol_own, sol_other, inter, gram, (in_north, in_south, in_west, in_east), grams)
    cross = jnp.zeros((1, K), F32)
    energy = jnp.zeros((1, K), F32)
    for s in range(2):
        jump0[s] = jumped[s]
        cross += jnp.sum(res[s] * jumped[s], axis=0, keepdims=True)
        energy += jnp.sum(jumped[s] * jumped[s], axis=0, keepdims=True)
    masks = [active_mask(sizes[s]) for s in range(2)]
    for s in range(2):
        copies[2 * s].wait()
        wide = dot(dbuf[s], jnp.concatenate(split2(jump0[s]), axis=1))
        prod[s] = masks[s] * (wide[:, :K] + wide[:, K:])
    for s in range(2):
        copies[2 * s + 1].wait()
        wide = dot(lbuf[s], jnp.concatenate(split2(prod[s]), axis=1))
        inner = jnp.transpose(wide[:, :K] + wide[:, K:])
        wide = dot(jnp.concatenate(split2(inner), axis=0), lbuf[s])
        inter1[s] = masks[s] * jnp.transpose(wide[:K] + wide[K:])
    rows = [jnp.zeros((1, K), F32)] * 2 + list(split3(cross)) + list(split3(energy))
    write_payload(pay, inter1, rows_of((16, K), rows))
    write_edges((north, south, west, east), inter1, None)


def third_kernel(sizes, sol_own, sol_other, inter, gram, in_north, in_south, in_west, in_east,
                 old_north, old_south, old_west, old_east, stats, res, search, jump0, prod,
                 res1, jump1, mult1, search1, pay):
    grams = [old_north[:, 2 * K :], old_south[:, 2 * K :], old_west[:, :, 2 * K :], old_east[:, :, 2 * K :]]
    again = jumps(sizes, sol_own, sol_other, inter, gram, (in_north, in_south, in_west, in_east), grams)
    step = stats[0:1] / (stats[1:2] + 1e-06)
    cross = jnp.zeros((1, K), F32)
    energy = jnp.zeros((1, K), F32)
    for s in range(2):
        res1[s] = res[s] - step * jump0[s]
        jumped = jump0[s] - step * again[s]
        jump1[s] = jumped
        mult1[s] = step * search[s]
        search1[s] = search[s] - step * prod[s]
        cross += jnp.sum(res1[s] * jumped, axis=0, keepdims=True)
        energy += jnp.sum(jumped * jumped, axis=0, keepdims=True)
    block = rows_of((8, K), [cross, energy])
    for dest in range(CS * XS):
        pay[dest] = block


def partial_kernel(rec, pay):
    total = sum(rec[b] for b in range(CS * XS))
    for dest in range(ZS * YS):
        pay[dest] = total


def last_kernel(rec, res1, jump1, mult1, search1, mult, res):
    total = sum(rec[b] for b in range(ZS * YS))
    step = total[0:1] / (total[1:2] + 1e-06)
    for s in range(2):
        mult[s] = mult1[s] + step * search1[s]
        res[s] = res1[s] - step * jump1[s]


def all_to_all(value, axes):
    return lax.all_to_all(value, axes, split_axis=0, concat_axis=0)


def swap(value):
    return lax.ppermute(value, "core", [(0, 1), (1, 0)])


def exchange(north, south, west, east):
    rows_up = [(i, i + 1) for i in range(ZS * CS - 1)]
    cols_up = [(j, j + 1) for j in range(SY - 1)]
    down = lambda pairs: [(b, a) for a, b in pairs]
    in_north = lax.ppermute(south, ("z", "core"), rows_up)
    in_south = lax.ppermute(north, ("z", "core"), down(rows_up))
    in_west = lax.ppermute(east, ("x", "y"), cols_up)
    in_east = lax.ppermute(west, ("x", "y"), down(cols_up))
    return in_north, in_south, in_west, in_east


def coarse_solution(own, snd):
    rcv = swap(snd)
    (pay,) = call(pair_sum_kernel, [((ZS, HALF + 16, K), BF16)], [VM] * 2)(own, rcv)
    rec = all_to_all(pay, "z")
    pay, stats = call(z_sum_kernel, [((SY, HALF, K), BF16), ((8, K), F32)], [VM])(rec)
    sol = all_to_all(pay, ("x", "y")).reshape(SY * HALF, K)
    return sol, swap(sol), stats


def local(factor_inv, dirichlet, coarse_inv, domain_sizes, corner_map, snow_level, pressure):
    factor = factor_inv.reshape(2, B, B)
    pre = dirichlet.reshape(2, B, B)
    sizes = domain_sizes.reshape(2)
    cm = corner_map.reshape(2, CORN)
    cmap = jnp.concatenate(
        [jnp.tile(cm, (1, 4)), jnp.tile(cm.reshape(1, 2 * CORN), (1, 2)), jnp.zeros((5, K), jnp.int32)], axis=0
    )
    whole = ((2, B, K), F32)
    bufs = [pltpu.VMEM((2, B, B), BF16), pltpu.VMEM((2, B, B), BF16), pltpu.SemaphoreType.DMA((4,))]

    def edge_outs(width):
        return [((E, width), BF16)] * 2 + [((2, E, width), BF16)] * 2

    res, search, inter, gram, pay, *edges = call(
        first_kernel,
        [whole, whole, whole, ((2, B, K), BF16), ((SY, ROWS, K), BF16)] + edge_outs(3 * K),
        [SM, VM, VM, VM, HB, HB],
        bufs,
    )(sizes, snow_level.reshape(2, B), cmap, pressure.reshape(2, B, K), pre, factor)
    arrived = exchange(*edges)
    rec = all_to_all(pay, ("x", "y"))
    own, snd, picked_inv = call(
        coarse_first_kernel,
        [((HALF + 8, K), F32)] * 2 + [((E, B), BF16)],
        [VM] * 2,
        [pltpu.VMEM((E, B), F32)],
    )(rec, coarse_inv)
    sol_own, sol_other, _ = coarse_solution(own, snd)
    jump0, prod, inter1, pay, *edges = call(
        second_kernel,
        [whole, whole, whole, ((SY, ROWS, K), BF16)] + edge_outs(2 * K),
        [SM] + [VM] * 9 + [HB] * 2,
        bufs,
    )(sizes, sol_own, sol_other, inter, gram, *arrived, res, pre, factor)
    arrived1 = exchange(*edges)
    rec = all_to_all(pay, ("x", "y"))
    own, snd = call(coarse_next_kernel, [((HALF + 8, K), F32)] * 2, [VM] * 2)(rec, picked_inv)
    sol_own, sol_other, stats = coarse_solution(own, snd)
    res1, jump1, mult1, search1, pay = call(
        third_kernel, [whole] * 4 + [((CS * XS, 8, K), F32)], [SM] + [VM] * 17
    )(sizes, sol_own, sol_other, inter1, gram, *arrived1, *arrived, stats, res, search, jump0, prod)
    rec = all_to_all(pay, ("core", "x"))
    (pay,) = call(partial_kernel, [((ZS * YS, 8, K), F32)], [VM])(rec)
    rec = all_to_all(pay, ("z", "y"))
    mult, res = call(last_kernel, [whole] * 2, [VM] * 5)(rec, res1, jump1, mult1, search1)
    return mult.reshape(2, 1, B, K), res.reshape(2, 1, B, K)


def solution(mesh):
    fine = Mesh(mesh.devices.reshape(ZS, CS, XS, YS), ("z", "core", "x", "y"))
    rows, cols = ("z", "core"), ("x", "y")
    return jax.shard_map(
        local,
        mesh=fine,
        in_specs=(
            P(rows, cols, None, None),
            P(rows, cols, None, None),
            P(cols, None),
            P(rows, cols),
            P(rows, cols, None),
            P(rows, cols, None),
            P(rows, cols, None, None),
        ),
        out_specs=(P(rows, cols, None, None), P(rows, cols, None, None)),
        check_vma=False,
    )
```

```python
import jax
import jax.numpy as jnp
from jax import lax
from jax.experimental import pallas as pl
from jax.experimental.pallas import tpu as pltpu
from jax.sharding import Mesh
from jax.sharding import PartitionSpec as P

B = 1024
E = 256
K = 128
CORN = 32
NC = 4096
GR = 32
GC = 16
ZS = 8
CS = 2
XS = 4
YS = 4
SY = XS * YS
STRIDE = B // CORN
ROWS = 80
HALF = 128
F32 = jnp.float32
BF16 = jnp.bfloat16
VMEM_LIMIT = 40 * 1024 * 1024

VM = pl.BlockSpec(memory_space=pltpu.VMEM)
SM = pl.BlockSpec(memory_space=pltpu.SMEM)
HB = pl.BlockSpec(memory_space=pltpu.HBM)
AN = pl.BlockSpec(memory_space=pl.ANY)


def dot(a, b):
    return jnp.dot(a, b, preferred_element_type=F32)


def iota(shape, dim):
    return lax.broadcasted_iota(jnp.int32, shape, dim)


def call(kernel, outs, in_specs, out_specs, scratch=(), aliases=None):
    run = pl.pallas_call(
        kernel,
        out_shape=[
            pltpu.HBM(shape, dtype) if spec is HB else jax.ShapeDtypeStruct(shape, dtype)
            for (shape, dtype), spec in zip(outs, out_specs)
        ],
        in_specs=in_specs,
        out_specs=out_specs,
        scratch_shapes=[pltpu.VMEM(*item) if isinstance(item, tuple) else item for item in scratch],
        input_output_aliases=aliases or {},
        compiler_params=pltpu.CompilerParams(vmem_limit_bytes=VMEM_LIMIT),
    )

    def placed(*args):
        return run(
            *[pltpu.with_memory_space_constraint(a, pltpu.HBM) if spec is HB else a for a, spec in zip(args, in_specs)]
        )

    return placed


class Copies:
    def __init__(self, sems):
        self.sems = sems
        self.count = 0
        self.out = []

    def fetch(self, source, target):
        copy = pltpu.make_async_copy(source, target, self.sems.at[self.count])
        self.count += 1
        copy.start()
        return copy

    def send(self, source, target):
        self.out.append(self.fetch(source, target))

    def finish(self):
        for copy in self.out:
            copy.wait()


def sems(count):
    return pltpu.SemaphoreType.DMA((count,))


def fetch_lower(copies, source, target):
    loads = []
    for block in range(B // E):
        rows, cols = pl.ds(block * E, E), pl.ds(0, (block + 1) * E)
        loads.append(copies.fetch(source.at[rows, cols], target.at[rows, cols]))
    return loads


def lower_times(matrix, loads, right):
    parts = []
    for block in range(B // E):
        loads[block].wait()
        width = (block + 1) * E
        parts.append(dot(matrix[block * E : width, :width], right[:width]))
    return jnp.concatenate(parts, axis=0)


def times_lower(left, matrix):
    parts = []
    for block in range(B // E):
        start = block * E
        parts.append(dot(left[:, start:], matrix[start:, start : start + E]))
    return jnp.concatenate(parts, axis=1)


def split2(value):
    high = value.astype(BF16)
    low = (value - high.astype(F32)).astype(BF16)
    return high, low


def split3(value):
    high, _ = split2(value)
    rest = value - high.astype(F32)
    mid, low = split2(rest)
    return high, mid, low


def active_mask(size):
    return ((iota((B, K), 0) & (E - 1)) < size).astype(F32)


def rows_of(shape, rows):
    index = iota(shape, 0)
    result = jnp.zeros(shape, F32)
    for number, row in enumerate(rows):
        result = jnp.where(index == number, jnp.broadcast_to(row.astype(F32), shape), result)
    return result


def send_payload(copies, pay, block, corners, tail):
    block[...] = jnp.concatenate([c.astype(BF16) for c in corners] + [tail.astype(BF16)], axis=0)
    for dest in range(SY):
        copies.send(block, pay.at[dest])


def send_edges(copies, bufs, targets, interface, extra):
    chip, far, near, other = bufs
    core = lax.axis_index("core")
    odd = lax.axis_index("y") & 1

    def packed(s, edge):
        rows = pl.ds(pl.multiple_of(edge * E, E), E)
        parts = list(split2(interface[s, rows, :]))
        if extra is not None:
            parts.append(extra[s, rows, :])
        return jnp.concatenate(parts, axis=1)

    chip[...] = packed(1 - core, 1 - core)
    far[...] = packed(core, core)
    for s in range(2):
        near[s] = packed(s, 3 - odd)
        other[s] = packed(s, 2 + odd)
    for source, target in zip(bufs, targets):
        copies.send(source, target)


def first_kernel(sizes_hbm, snow_hbm, cmap_hbm, press_hbm, dir_hbm, fac_hbm,
                 res, search, half, pay, dbuf, lbuf, press, resv, searchv, halfv, block, snow, cmap, sizes, sem):
    copies = Copies(sem)
    small = [copies.fetch(a, b) for a, b in ((sizes_hbm, sizes), (snow_hbm, snow), (cmap_hbm, cmap))]
    load = copies.fetch(press_hbm, press)
    dirs, facs = [], []
    for s in range(2):
        dirs.append(copies.fetch(dir_hbm.at[s, 0], dbuf.at[s]))
    for s in range(2):
        facs.append(fetch_lower(copies, fac_hbm.at[s, 0], lbuf.at[s]))
    grid_row = lax.axis_index("z") * (2 * CS) + lax.axis_index("core") * 2
    grid_col = lax.axis_index("x") * YS + lax.axis_index("y")
    lane = iota((B, K), 1)
    for copy in small:
        copy.wait()
    masks = [active_mask(sizes[s]) for s in range(2)]
    pick_col = jnp.where((iota((B, K), 0) == lane * STRIDE) & (lane < CORN), 1.0, 0.0).astype(BF16)
    columns = []
    for s in range(2):
        place = jnp.full((1, B), grid_row + s + grid_col, jnp.int32).astype(F32)
        drift = 1.0 + 2.0 * place / (GR + GC - 2)
        depth = 0.5 + 0.25 * snow[s].astype(F32)
        columns.append([jnp.transpose(jnp.broadcast_to(row, (K, B))) for row in (depth, drift)])
    load.wait()
    for s in range(2):
        resv[s] = press[s, 0].astype(F32) * columns[s][0] * columns[s][1] * masks[s]
        copies.send(resv.at[s], res.at[s])
    for s in range(2):
        dirs[s].wait()
        searchv[s] = masks[s] * dot(dbuf[s], resv[s].astype(BF16))
        copies.send(searchv.at[s], search.at[s])
    corners = []
    for s in range(2):
        right = jnp.concatenate([searchv[s].astype(BF16), pick_col], axis=1)
        wide = lower_times(lbuf.at[s], facs[s], right)
        turned = jnp.transpose(wide).astype(BF16)
        halfv[s] = turned
        copies.send(halfv.at[s], half.at[s])
        rows = dot(turned[K : K + CORN], wide[:, :K].astype(BF16))
        corners.append(corner_mask(sizes[s]) * rows)
    cm = two_rows(cmap)
    tail = rows_of((16, K), [(cm >> 8).astype(F32), (cm & 255).astype(F32)])
    send_payload(copies, pay, block, corners, tail)
    copies.finish()


def corner_mask(size):
    return (((iota((CORN, K), 0) * STRIDE) & (E - 1)) < size).astype(F32)


def tiled_row(row):
    return jnp.concatenate([row] * (K // CORN), axis=1)


def two_rows(cmap):
    lane = iota((1, K), 1)
    return jnp.where((lane & CORN) == 0, tiled_row(cmap[0]), tiled_row(cmap[1]))


def back_first_kernel(sizes, cmap, half_hbm, fac_hbm, inter, gram, chip, far, near, other,
                      half, lbuf, interv, gramv, e0, e1, e2, e3, sem):
    copies = Copies(sem)
    facs, halves_in = [], []
    for s in range(2):
        halves_in.append(copies.fetch(half_hbm.at[s], half.at[s]))
        facs.append(fetch_lower(copies, fac_hbm.at[s, 0], lbuf.at[s]))
    lane = iota((B, K), 1)
    for s in range(2):
        mask = active_mask(sizes[s])
        square = jnp.transpose(jnp.broadcast_to(tiled_row(cmap[s]), (K, K)))
        column = jnp.concatenate([square] * (B // K), axis=0)
        digits = jnp.where(lane < 96, column >> 8, column & 255).astype(F32)
        halves_in[s].wait()
        for load in facs[s]:
            load.wait()
        back = jnp.transpose(times_lower(half.at[s], lbuf.at[s]))
        interv[s] = mask * back[:, :K]
        copies.send(interv.at[s], inter.at[s])
        ghigh, glow = split2(mask * back[:, K:])
        low_moved = pltpu.roll(glow.astype(F32), CORN, axis=1)
        gramv[s] = jnp.where(
            lane < CORN, ghigh.astype(F32), jnp.where(lane < 2 * CORN, low_moved, digits)
        ).astype(BF16)
        copies.send(gramv.at[s], gram.at[s])
    send_edges(copies, (e0, e1, e2, e3), (chip, far, near, other), interv, gramv)
    copies.finish()


def coarse_rows(rec):
    return jnp.concatenate([rec[b, 0:64, :] for b in range(SY)], axis=0)


def halves(value, stats, own, snd):
    mine = lax.axis_index("core") == 0
    tail = rows_of((8, K), stats)
    own[0:HALF] = jnp.where(mine, value[:HALF], value[HALF:])
    snd[0:HALF] = jnp.where(mine, value[HALF:], value[:HALF])
    own[HALF : HALF + 8] = tail
    snd[HALF : HALF + 8] = tail


def coarse_first_kernel(rec, coarse_hbm, _, own, snd, picked_inv, coarse, matrix, hot, sem):
    copies = Copies(sem)
    load = copies.fetch(coarse_hbm, coarse)
    lane = iota((1, K), 1)
    tails = [rec[b, 64:80, :].astype(F32) for b in range(SY)]

    def row(number):
        parts = [
            jnp.where(lane < 64, tails[2 * m][number : number + 1], tails[2 * m + 1][number : number + 1])
            for m in range(SY // 2)
        ]
        return jnp.concatenate(parts, axis=1)

    high, low = row(0), row(1)
    low_hot = jnp.where(iota((E, B), 0) == low.astype(jnp.int32), 1.0, 0.0).astype(BF16)
    high_hot = jnp.where(iota((NC // E, B), 0) == high.astype(jnp.int32), 1.0, 0.0).astype(BF16)
    for digit in range(NC // E):
        hot[digit * E : (digit + 1) * E] = low_hot * high_hot[digit : digit + 1]
    load.wait()
    matrix[...] = dot(coarse[...], hot[...]).astype(BF16)
    copies.send(matrix, picked_inv)
    halves(dot(matrix[...], coarse_rows(rec)), [], own, snd)
    copies.finish()


def coarse_next_kernel(rec, picked_inv, _, own, snd):
    value = dot(picked_inv[...], coarse_rows(rec))
    tails = sum(rec[b, 64:80, :].astype(F32) for b in range(SY))
    stats = [tails[q : q + 1] + tails[q + 1 : q + 2] + tails[q + 2 : q + 3] for q in (2, 5)]
    halves(value, stats, own, snd)


def pair_sum_kernel(own, rcv, pay, block, sem):
    copies = Copies(sem)
    total = own[...] + rcv[...]
    rows = []
    for q in range(2):
        rows += list(split3(total[HALF + q : HALF + q + 1]))
    tail = rows_of((16, K), rows).astype(BF16)
    block[...] = jnp.concatenate([total[:HALF].astype(BF16), tail], axis=0)
    for dest in range(ZS):
        copies.send(block, pay.at[dest])
    copies.finish()


def z_sum_kernel(rec, _, __, pay, stats, block, sem):
    copies = Copies(sem)
    total = sum(rec[z].astype(F32) for z in range(ZS))
    block[...] = total[:HALF].astype(BF16)
    for dest in range(SY):
        copies.send(block, pay.at[dest])
    rows = total[HALF:]
    stats[...] = rows_of(
        (8, K), [rows[q : q + 1] + rows[q + 1 : q + 2] + rows[q + 2 : q + 3] for q in (0, 3)]
    )
    copies.finish()


def tie_kernel(source, _, __, target):
    pass


def jumps(sizes, sol_own, sol_other, inter, gram, edges, grams):
    core = lax.axis_index("core")
    odd = lax.axis_index("y") & 1
    chip, far, near, other = edges
    gchip, gfar, gnear, gother = grams

    def ordered(flag, a, b):
        return jnp.where(flag == 0, b, a), jnp.where(flag == 0, a, b)

    north, south = ordered(core, chip[...], far[...])
    gnorth, gsouth = ordered(core, gchip, gfar)
    west, east = ordered(odd, near[...], other[...])
    gwest, geast = ordered(odd, gnear, gother)
    gram_edges = [gram[0, 0:CORN, :], gram[1, 0:CORN, :], gnorth[0:CORN], gsouth[0:CORN]]
    gram_edges += [g[s, 0:CORN, :] for g in (gwest, geast) for s in range(2)]
    digits = jnp.concatenate(gram_edges, axis=0).astype(F32)
    cm = digits[:, 64:65].astype(jnp.int32) * 256 + digits[:, 96:97].astype(jnp.int32)
    half = ((cm >> 7) & 1) ^ core
    place = half * 2048 + (cm >> 8) * HALF + (cm & (HALF - 1))
    hot = jnp.where(iota((8 * CORN, NC), 1) == place, 1.0, 0.0).astype(BF16)
    picks = (dot(hot[:, :2048], sol_own[...]) + dot(hot[:, 2048:], sol_other[...])).astype(BF16)
    zero = jnp.zeros((2 * CORN, K), BF16)

    def stacked(number):
        rows = picks[number * CORN : (number + 1) * CORN]
        return jnp.concatenate([rows, rows, zero], axis=0)

    full = [inter[s] + dot(gram[s], stacked(s)) for s in range(2)]

    def arrived(edge, gedge, number):
        return edge[:, :K].astype(F32) + edge[:, K : 2 * K].astype(F32) + dot(gedge, stacked(number))

    above = [arrived(north, gnorth, 2), full[0][E : 2 * E]]
    below = [full[1][0:E], arrived(south, gsouth, 3)]
    left = [arrived(west[s], gwest[s], 4 + s) for s in range(2)]
    right = [arrived(east[s], geast[s], 6 + s) for s in range(2)]
    return [
        active_mask(sizes[s]) * (full[s] - jnp.concatenate([above[s], below[s], left[s], right[s]], axis=0))
        for s in range(2)
    ]


def edge_grams(chip, far, near, other):
    return chip[:, 2 * K :], far[:, 2 * K :], near[:, :, 2 * K :], other[:, :, 2 * K :]


def second_kernel(sizes, sol_own, sol_other, inter_hbm, gram_hbm, chip_hbm, far_hbm, near_hbm, other_hbm,
                  res_hbm, dir_hbm, fac_hbm, half_hbm,
                  jump0, prod, half, pay,
                  inter, gram, chip, far, near, other, res, dbuf, lbuf, corner, jumpv, prodv, halfv, block, sem):
    copies = Copies(sem)
    edges = (chip, far, near, other)
    loads = [copies.fetch(gram_hbm, gram)]
    loads += [copies.fetch(a, b) for a, b in zip((chip_hbm, far_hbm, near_hbm, other_hbm), edges)]
    loads.append(copies.fetch(inter_hbm, inter))
    res_in = copies.fetch(res_hbm, res)
    dirs = [copies.fetch(dir_hbm.at[s, 0], dbuf.at[s]) for s in range(2)]
    facs = [fetch_lower(copies, fac_hbm.at[s, 0], lbuf.at[s]) for s in range(2)]
    corner_in = copies.fetch(half_hbm.at[:, pl.ds(K, CORN), :], corner)
    for load in loads:
        load.wait()
    jumped = jumps(sizes, sol_own, sol_other, inter, gram, edges, edge_grams(*edges))
    res_in.wait()
    cross = jnp.zeros((1, K), F32)
    energy = jnp.zeros((1, K), F32)
    for s in range(2):
        jumpv[s] = jumped[s]
        copies.send(jumpv.at[s], jump0.at[s])
        cross += jnp.sum(res[s] * jumped[s], axis=0, keepdims=True)
        energy += jnp.sum(jumped[s] * jumped[s], axis=0, keepdims=True)
    for s in range(2):
        dirs[s].wait()
        wide = dot(dbuf[s], jnp.concatenate(split2(jumpv[s]), axis=1))
        prodv[s] = active_mask(sizes[s]) * (wide[:, :K] + wide[:, K:])
        copies.send(prodv.at[s], prod.at[s])
    corner_in.wait()
    corners = []
    for s in range(2):
        wide = lower_times(lbuf.at[s], facs[s], jnp.concatenate(split2(prodv[s]), axis=1))
        inner = wide[:, :K] + wide[:, K:]
        halfv[s] = jnp.concatenate(split2(jnp.transpose(inner)), axis=0)
        copies.send(halfv.at[s], half.at[s])
        rows = dot(corner[s], jnp.concatenate(split2(inner), axis=1))
        corners.append(corner_mask(sizes[s]) * (rows[:, :K] + rows[:, K:]))
    rows = [jnp.zeros((1, K), F32)] * 2 + list(split3(cross)) + list(split3(energy))
    send_payload(copies, pay, block, corners, rows_of((16, K), rows))
    copies.finish()


def back_next_kernel(sizes, half_hbm, fac_hbm, inter, chip, far, near, other,
                     half, lbuf, interv, e0, e1, e2, e3, sem):
    copies = Copies(sem)
    facs, halves_in = [], []
    for s in range(2):
        halves_in.append(copies.fetch(half_hbm.at[s], half.at[s]))
        facs.append(fetch_lower(copies, fac_hbm.at[s, 0], lbuf.at[s]))
    for s in range(2):
        halves_in[s].wait()
        for load in facs[s]:
            load.wait()
        wide = times_lower(half.at[s], lbuf.at[s])
        interv[s] = active_mask(sizes[s]) * jnp.transpose(wide[:K] + wide[K:])
        copies.send(interv.at[s], inter.at[s])
    send_edges(copies, (e0, e1, e2, e3), (chip, far, near, other), interv, None)
    copies.finish()


def third_kernel(sizes, sol_own, sol_other, stats, inter_hbm, gram_hbm, chip_hbm, far_hbm, near_hbm, other_hbm,
                 old_chip, old_far, old_near, old_other, res_hbm, jump_hbm,
                 res1, jump1, pay,
                 inter, gram, chip, far, near, other, gchip, gfar, gnear, gother, res, jump0, sem):
    copies = Copies(sem)
    edges = (chip, far, near, other)
    grams = (gchip, gfar, gnear, gother)
    width = pl.ds(2 * K, K)
    loads = [copies.fetch(gram_hbm, gram)]
    loads += [copies.fetch(a.at[:, width], b) for a, b in zip((old_chip, old_far), grams[:2])]
    loads += [copies.fetch(a.at[:, :, width], b) for a, b in zip((old_near, old_other), grams[2:])]
    loads += [copies.fetch(a, b) for a, b in zip((chip_hbm, far_hbm, near_hbm, other_hbm), edges)]
    loads.append(copies.fetch(inter_hbm, inter))
    late = [copies.fetch(res_hbm, res), copies.fetch(jump_hbm, jump0)]
    for load in loads:
        load.wait()
    again = jumps(sizes, sol_own, sol_other, inter, gram, edges, tuple(g[...] for g in grams))
    for load in late:
        load.wait()
    step = stats[0:1] / (stats[1:2] + 1e-06)
    cross = jnp.zeros((1, K), F32)
    energy = jnp.zeros((1, K), F32)
    for s in range(2):
        before = res[s] - step * jump0[s]
        jumped = jump0[s] - step * again[s]
        res1[s] = before
        jump1[s] = jumped
        cross += jnp.sum(before * jumped, axis=0, keepdims=True)
        energy += jnp.sum(jumped * jumped, axis=0, keepdims=True)
    block = rows_of((8, K), [cross, energy])
    for dest in range(CS * XS):
        pay[dest] = block


def partial_kernel(rec, pay):
    total = sum(rec[b] for b in range(CS * XS))
    for dest in range(ZS * YS):
        pay[dest] = total


def last_kernel(rec, stats, res1, jump1, search, prod, mult, res, multv, resv, sem):
    copies = Copies(sem)
    total = sum(rec[b] for b in range(ZS * YS))
    first = stats[0:1] / (stats[1:2] + 1e-06)
    step = total[0:1] / (total[1:2] + 1e-06)
    for s in range(2):
        multv[s] = first * search[s] + step * (search[s] - first * prod[s])
        copies.send(multv.at[s], mult.at[s])
        resv[s] = res1[s] - step * jump1[s]
        copies.send(resv.at[s], res.at[s])
    copies.finish()


def all_to_all(value, axes):
    return lax.all_to_all(value, axes, split_axis=0, concat_axis=0)


def swap(value):
    return lax.ppermute(value, "core", [(0, 1), (1, 0)])


def exchange(chip, far, near, other):
    even = [(i, i ^ 1) for i in range(16)]
    odd = [(i, i + 1) for i in range(1, 15, 2)] + [(i + 1, i) for i in range(1, 15, 2)]
    rows, cols = ("z", "core"), ("x", "y")
    return (
        lax.ppermute(chip, rows, even),
        lax.ppermute(far, rows, odd),
        lax.ppermute(near, cols, even),
        lax.ppermute(other, cols, odd),
    )


def coarse_solution(own, snd, arrived):
    pay3 = ((ZS, HALF + 16, K), BF16)
    rcv = swap(snd)
    (pay,) = call(pair_sum_kernel, [pay3], [VM] * 2, [HB], [(pay3[0][1:], BF16), sems(ZS)])(own, rcv)
    rec = all_to_all(pay, "z")
    pay, stats = call(
        z_sum_kernel,
        [((SY, HALF, K), BF16), ((8, K), F32)],
        [VM, HB, HB],
        [HB, VM],
        [((HALF, K), BF16), sems(SY)],
    )(rec, *arrived[2:])
    sol = all_to_all(pay, ("x", "y"))
    (sol,) = call(tie_kernel, [((SY, HALF, K), BF16)], [AN] + [HB] * 2, [AN], aliases={0: 0})(sol, *arrived[:2])
    sol = sol.reshape(SY * HALF, K)
    return sol, swap(sol), stats


def local(factor, pre, coarse_inv, sizes, cmap, snow_level, pressure):
    sizes = sizes.reshape(2)
    whole = ((2, B, K), F32)
    gramed = ((2, B, K), BF16)
    halved = ((2, 2 * K, B), BF16)
    square = ((2, B, B), BF16)
    payload = ((SY, ROWS, K), BF16)
    block = (payload[0][1:], BF16)
    sent = [((HALF + 8, K), F32)] * 2

    def edges_of(width):
        return [((E, width), BF16)] * 2 + [((2, E, width), BF16)] * 2

    res, search, half, pay = call(
        first_kernel,
        [whole, whole, halved, payload],
        [HB] * 6,
        [HB] * 4,
        [square, square, ((2, 1, B, K), BF16), whole, whole, halved, block]
        + [((2, 1, B), jnp.int32), ((2, 1, CORN), jnp.int32), pltpu.SMEM((2,), jnp.int32), sems(20 + SY)],
    )(sizes, snow_level, cmap, pressure, pre, factor)
    rec = all_to_all(pay, ("x", "y"))
    wide = edges_of(3 * K)
    inter, gram, *edges = call(
        back_first_kernel,
        [whole, gramed] + wide,
        [SM, VM, HB, HB],
        [HB] * 6,
        [halved, square, whole, gramed] + wide + [sems(18)],
    )(sizes, cmap, half, factor)
    arrived = exchange(*edges)
    own, snd, picked_inv = call(
        coarse_first_kernel,
        sent + [((E, B), BF16)],
        [VM, HB, HB],
        [VM, VM, HB],
        [((E, NC), BF16), ((E, B), BF16), ((NC, B), BF16), sems(2)],
    )(rec, coarse_inv, gram)
    sol_own, sol_other, _ = coarse_solution(own, snd, arrived)
    jump0, prod, half1, pay = call(
        second_kernel,
        [whole, whole, halved, payload],
        [SM, VM, VM] + [HB] * 10,
        [HB] * 4,
        [whole, gramed] + wide + [whole, square, square, ((2, CORN, B), BF16), whole, whole, halved, block, sems(24 + SY)],
    )(sizes, sol_own, sol_other, inter, gram, *arrived, res, pre, factor, half)
    rec = all_to_all(pay, ("x", "y"))
    slim = edges_of(2 * K)
    inter1, *edges = call(
        back_next_kernel,
        [whole] + slim,
        [SM] + [HB] * 2,
        [HB] * 5,
        [halved, square, whole] + slim + [sems(16)],
    )(sizes, half1, factor)
    arrived1 = exchange(*edges)
    own, snd = call(coarse_next_kernel, sent, [VM] * 2 + [HB], [VM] * 2)(rec, picked_inv, inter1)
    sol_own, sol_other, stats = coarse_solution(own, snd, arrived1)
    res1, jump1, pay = call(
        third_kernel,
        [whole] * 2 + [((CS * XS, 8, K), F32)],
        [SM] + [VM] * 3 + [HB] * 12,
        [VM] * 3,
        [whole, gramed] + slim + edges_of(K) + [whole, whole, sems(12)],
    )(sizes, sol_own, sol_other, stats, inter1, gram, *arrived1, *arrived, res, jump0)
    rec = all_to_all(pay, ("core", "x"))
    (pay,) = call(partial_kernel, [((ZS * YS, 8, K), F32)], [VM], [VM])(rec)
    rec = all_to_all(pay, ("z", "y"))
    mult, res = call(last_kernel, [whole] * 2, [VM] * 6, [HB] * 2, [whole, whole, sems(4)])(
        rec, stats, res1, jump1, search, prod
    )
    return mult.reshape(2, 1, B, K), res.reshape(2, 1, B, K)


def solution(mesh):
    fine = Mesh(mesh.devices.reshape(ZS, CS, XS, YS), ("z", "core", "x", "y"))
    rows, cols = ("z", "core"), ("x", "y")
    return jax.shard_map(
        local,
        mesh=fine,
        in_specs=(
            P(rows, cols, None, None),
            P(rows, cols, None, None),
            P(cols, None),
            P(rows, cols),
            P(rows, cols, None),
            P(rows, cols, None),
            P(rows, cols, None, None),
        ),
        out_specs=(P(rows, cols, None, None), P(rows, cols, None, None)),
        check_vma=False,
    )
```

```python
import jax
import jax.numpy as jnp
from jax import lax
from jax.experimental import pallas as pl
from jax.experimental.pallas import tpu as pltpu
from jax.sharding import Mesh
from jax.sharding import PartitionSpec as P

B = 1024
E = 256
K = 128
CORN = 32
NC = 4096
GR = 32
GC = 16
ZS = 8
CS = 2
XS = 4
YS = 4
SY = XS * YS
STRIDE = B // CORN
ROWS = 80
HALF = 128
F32 = jnp.float32
BF16 = jnp.bfloat16
VMEM_LIMIT = 40 * 1024 * 1024

VM = pl.BlockSpec(memory_space=pltpu.VMEM)
SM = pl.BlockSpec(memory_space=pltpu.SMEM)
HB = pl.BlockSpec(memory_space=pltpu.HBM)
AN = pl.BlockSpec(memory_space=pl.ANY)


def dot(a, b):
    return jnp.dot(a, b, preferred_element_type=F32)


def iota(shape, dim):
    return lax.broadcasted_iota(jnp.int32, shape, dim)


def call(kernel, outs, in_specs, out_specs, scratch=(), aliases=None):
    run = pl.pallas_call(
        kernel,
        out_shape=[
            pltpu.HBM(shape, dtype) if spec is HB else jax.ShapeDtypeStruct(shape, dtype)
            for (shape, dtype), spec in zip(outs, out_specs)
        ],
        in_specs=in_specs,
        out_specs=out_specs,
        scratch_shapes=[pltpu.VMEM(*item) if isinstance(item, tuple) else item for item in scratch],
        input_output_aliases=aliases or {},
        compiler_params=pltpu.CompilerParams(vmem_limit_bytes=VMEM_LIMIT),
    )

    def placed(*args):
        return run(
            *[pltpu.with_memory_space_constraint(a, pltpu.HBM) if spec is HB else a for a, spec in zip(args, in_specs)]
        )

    return placed


class Copies:
    def __init__(self, sems):
        self.sems = sems
        self.count = 0
        self.out = []

    def fetch(self, source, target):
        copy = pltpu.make_async_copy(source, target, self.sems.at[self.count])
        self.count += 1
        copy.start()
        return copy

    def send(self, source, target):
        self.out.append(self.fetch(source, target))

    def finish(self):
        for copy in self.out:
            copy.wait()


def sems(count):
    return pltpu.SemaphoreType.DMA((count,))


def fetch_lower(copies, source, target):
    loads = []
    for block in range(B // E):
        rows, cols = pl.ds(block * E, E), pl.ds(0, (block + 1) * E)
        loads.append(copies.fetch(source.at[rows, cols], target.at[rows, cols]))
    return loads


def dot_turned(a, b):
    return lax.dot_general(a, b, (((1,), (1,)), ((), ())), preferred_element_type=F32)


def times_lower_turned(left, matrix, loads):
    for load in loads:
        load.wait()
    parts = []
    for block in range(B // E):
        width = (block + 1) * E
        parts.append(dot_turned(left[:, :width], matrix[block * E : width, :width]))
    return jnp.concatenate(parts, axis=1)


def times_lower(left, matrix):
    parts = []
    for block in range(B // E):
        start = block * E
        parts.append(dot(left[:, start:], matrix[start:, start : start + E]))
    return jnp.concatenate(parts, axis=1)


def split2(value):
    high = value.astype(BF16)
    low = (value - high.astype(F32)).astype(BF16)
    return high, low


def split3(value):
    high, _ = split2(value)
    rest = value - high.astype(F32)
    mid, low = split2(rest)
    return high, mid, low


def active_mask(size):
    return ((iota((B, K), 0) & (E - 1)) < size).astype(F32)


def rows_of(shape, rows):
    index = iota(shape, 0)
    result = jnp.zeros(shape, F32)
    for number, row in enumerate(rows):
        result = jnp.where(index == number, jnp.broadcast_to(row.astype(F32), shape), result)
    return result


def send_payload(copies, pay, block, corners, tail):
    block[...] = jnp.concatenate([c.astype(BF16) for c in corners] + [tail.astype(BF16)], axis=0)
    for dest in range(SY):
        copies.send(block, pay.at[dest])


def send_edges(copies, bufs, targets, interface, extra):
    chip, far, near, other = bufs
    core = lax.axis_index("core")
    odd = lax.axis_index("y") & 1

    def packed(s, edge):
        rows = pl.ds(pl.multiple_of(edge * E, E), E)
        parts = [interface[s, rows, :].astype(BF16)]
        if extra is not None:
            parts.append(extra[s, rows, :])
        return jnp.concatenate(parts, axis=1)

    chip[...] = packed(1 - core, 1 - core)
    far[...] = packed(core, core)
    for s in range(2):
        near[s] = packed(s, 3 - odd)
        other[s] = packed(s, 2 + odd)
    for source, target in zip(bufs, targets):
        copies.send(source, target)


def first_kernel(sizes_hbm, snow_hbm, cmap_hbm, press_hbm, dir_hbm, fac_hbm,
                 res, search, half, pay, dbuf, lbuf, press, resv, searchv, halfv, block, snow, cmap, sizes, sem):
    copies = Copies(sem)
    small = [copies.fetch(a, b) for a, b in ((sizes_hbm, sizes), (snow_hbm, snow), (cmap_hbm, cmap))]
    load = copies.fetch(press_hbm, press)
    dirs, facs = [], []
    for s in range(2):
        dirs.append(copies.fetch(dir_hbm.at[s, 0], dbuf.at[s]))
    for s in range(2):
        facs.append(fetch_lower(copies, fac_hbm.at[s, 0], lbuf.at[s]))
    grid_row = lax.axis_index("z") * (2 * CS) + lax.axis_index("core") * 2
    grid_col = lax.axis_index("x") * YS + lax.axis_index("y")
    for copy in small:
        copy.wait()
    masks = [active_mask(sizes[s]) for s in range(2)]
    pick = jnp.where(iota((CORN, B), 1) == iota((CORN, B), 0) * STRIDE, 1.0, 0.0).astype(BF16)
    columns = []
    for s in range(2):
        place = jnp.full((1, B), grid_row + s + grid_col, jnp.int32).astype(F32)
        drift = 1.0 + 2.0 * place / (GR + GC - 2)
        depth = 0.5 + 0.25 * snow[s].astype(F32)
        columns.append([jnp.transpose(jnp.broadcast_to(row, (K, B))) for row in (depth, drift)])
    load.wait()
    for s in range(2):
        resv[s] = press[s, 0].astype(F32) * columns[s][0] * columns[s][1] * masks[s]
        copies.send(resv.at[s], res.at[s])
    for s in range(2):
        dirs[s].wait()
        searchv[s] = masks[s] * dot(dbuf[s], resv[s].astype(BF16))
        copies.send(searchv.at[s], search.at[s])
    corners = []
    for s in range(2):
        left = jnp.concatenate([jnp.transpose(searchv[s]).astype(BF16), pick], axis=0)
        turned = times_lower_turned(left, lbuf.at[s], facs[s]).astype(BF16)
        halfv[s] = turned
        copies.send(halfv.at[s], half.at[s])
        rows = dot_turned(turned[K:], turned[:K])
        corners.append(corner_mask(sizes[s]) * rows)
    cm = two_rows(cmap)
    tail = rows_of((16, K), [(cm >> 8).astype(F32), (cm & 255).astype(F32)])
    send_payload(copies, pay, block, corners, tail)
    copies.finish()


def corner_mask(size):
    return (((iota((CORN, K), 0) * STRIDE) & (E - 1)) < size).astype(F32)


def tiled_row(row):
    return jnp.concatenate([row] * (K // CORN), axis=1)


def two_rows(cmap):
    lane = iota((1, K), 1)
    return jnp.where((lane & CORN) == 0, tiled_row(cmap[0]), tiled_row(cmap[1]))


def back_first_kernel(sizes, cmap, half_hbm, fac_hbm, inter, gram, chip, far, near, other,
                      half, lbuf, interv, gramv, e0, e1, e2, e3, sem):
    copies = Copies(sem)
    facs, halves_in = [], []
    for s in range(2):
        halves_in.append(copies.fetch(half_hbm.at[s], half.at[s]))
        facs.append(fetch_lower(copies, fac_hbm.at[s, 0], lbuf.at[s]))
    lane = iota((B, K), 1)
    for s in range(2):
        mask = active_mask(sizes[s])
        square = jnp.transpose(jnp.broadcast_to(tiled_row(cmap[s]), (K, K)))
        column = jnp.concatenate([square] * (B // K), axis=0)
        digits = jnp.where(lane < 96, column >> 8, column & 255).astype(F32)
        halves_in[s].wait()
        for load in facs[s]:
            load.wait()
        back = jnp.transpose(times_lower(half.at[s], lbuf.at[s]))
        interv[s] = mask * back[:, :K]
        copies.send(interv.at[s], inter.at[s])
        ghigh, glow = split2(mask * jnp.concatenate([back[:, K:], jnp.zeros((B, K - CORN), F32)], axis=1))
        low_moved = pltpu.roll(glow.astype(F32), CORN, axis=1)
        gramv[s] = jnp.where(
            lane < CORN, ghigh.astype(F32), jnp.where(lane < 2 * CORN, low_moved, digits)
        ).astype(BF16)
        copies.send(gramv.at[s], gram.at[s])
    send_edges(copies, (e0, e1, e2, e3), (chip, far, near, other), interv, gramv)
    copies.finish()


def coarse_rows(rec):
    return jnp.concatenate([rec[b, 0:64, :] for b in range(SY)], axis=0)


def halves(value, stats, own, snd):
    mine = lax.axis_index("core") == 0
    tail = rows_of((8, K), stats)
    own[0:HALF] = jnp.where(mine, value[:HALF], value[HALF:])
    snd[0:HALF] = jnp.where(mine, value[HALF:], value[:HALF])
    own[HALF : HALF + 8] = tail
    snd[HALF : HALF + 8] = tail


def coarse_first_kernel(rec, coarse_hbm, _, own, snd, picked_inv, coarse, matrix, hot, sem):
    copies = Copies(sem)
    load = copies.fetch(coarse_hbm, coarse)
    lane = iota((1, K), 1)
    tails = [rec[b, 64:80, :].astype(F32) for b in range(SY)]

    def row(number):
        parts = [
            jnp.where(lane < 64, tails[2 * m][number : number + 1], tails[2 * m + 1][number : number + 1])
            for m in range(SY // 2)
        ]
        return jnp.concatenate(parts, axis=1)

    high, low = row(0), row(1)
    low_hot = jnp.where(iota((E, B), 0) == low.astype(jnp.int32), 1.0, 0.0).astype(BF16)
    high_hot = jnp.where(iota((NC // E, B), 0) == high.astype(jnp.int32), 1.0, 0.0).astype(BF16)
    for digit in range(NC // E):
        hot[digit * E : (digit + 1) * E] = low_hot * high_hot[digit : digit + 1]
    load.wait()
    matrix[...] = dot(coarse[...], hot[...]).astype(BF16)
    copies.send(matrix, picked_inv)
    halves(dot(matrix[...], coarse_rows(rec)), [], own, snd)
    copies.finish()


def coarse_next_kernel(rec, picked_inv, _, own, snd):
    value = dot(picked_inv[...], coarse_rows(rec))
    tails = sum(rec[b, 64:80, :].astype(F32) for b in range(SY))
    stats = [tails[q : q + 1] + tails[q + 1 : q + 2] + tails[q + 2 : q + 3] for q in (2, 5)]
    halves(value, stats, own, snd)


def pair_sum_kernel(own, rcv, pay, block, sem):
    copies = Copies(sem)
    total = own[...] + rcv[...]
    rows = []
    for q in range(2):
        rows += list(split3(total[HALF + q : HALF + q + 1]))
    tail = rows_of((16, K), rows).astype(BF16)
    block[...] = jnp.concatenate([total[:HALF].astype(BF16), tail], axis=0)
    for dest in range(ZS):
        copies.send(block, pay.at[dest])
    copies.finish()


def z_sum_kernel(rec, _, __, pay, stats, block, sem):
    copies = Copies(sem)
    total = sum(rec[z].astype(F32) for z in range(ZS))
    block[...] = total[:HALF].astype(BF16)
    for dest in range(SY):
        copies.send(block, pay.at[dest])
    rows = total[HALF:]
    stats[...] = rows_of(
        (8, K), [rows[q : q + 1] + rows[q + 1 : q + 2] + rows[q + 2 : q + 3] for q in (0, 3)]
    )
    copies.finish()


def tie_kernel(source, _, __, target):
    pass


def jumps(sizes, sol_own, sol_other, inter, gram, edges, grams):
    core = lax.axis_index("core")
    odd = lax.axis_index("y") & 1
    chip, far, near, other = edges
    gchip, gfar, gnear, gother = grams

    def ordered(flag, a, b):
        return jnp.where(flag == 0, b, a), jnp.where(flag == 0, a, b)

    north, south = ordered(core, chip[...], far[...])
    gnorth, gsouth = ordered(core, gchip, gfar)
    west, east = ordered(odd, near[...], other[...])
    gwest, geast = ordered(odd, gnear, gother)
    gram_edges = [gram[0, 0:CORN, :], gram[1, 0:CORN, :], gnorth[0:CORN], gsouth[0:CORN]]
    gram_edges += [g[s, 0:CORN, :] for g in (gwest, geast) for s in range(2)]
    digits = jnp.concatenate(gram_edges, axis=0).astype(F32)
    cm = digits[:, 64:65].astype(jnp.int32) * 256 + digits[:, 96:97].astype(jnp.int32)
    half = ((cm >> 7) & 1) ^ core
    place = half * 2048 + (cm >> 8) * HALF + (cm & (HALF - 1))
    hot = jnp.where(iota((8 * CORN, NC), 1) == place, 1.0, 0.0).astype(BF16)
    picks = (dot(hot[:, :2048], sol_own[...]) + dot(hot[:, 2048:], sol_other[...])).astype(BF16)
    zero = jnp.zeros((2 * CORN, K), BF16)

    def stacked(number):
        rows = picks[number * CORN : (number + 1) * CORN]
        return jnp.concatenate([rows, rows, zero], axis=0)

    full = [inter[s] + dot(gram[s], stacked(s)) for s in range(2)]

    def arrived(edge, gedge, number):
        return edge[:, :K].astype(F32) + dot(gedge, stacked(number))

    above = [arrived(north, gnorth, 2), full[0][E : 2 * E]]
    below = [full[1][0:E], arrived(south, gsouth, 3)]
    left = [arrived(west[s], gwest[s], 4 + s) for s in range(2)]
    right = [arrived(east[s], geast[s], 6 + s) for s in range(2)]
    return [
        active_mask(sizes[s]) * (full[s] - jnp.concatenate([above[s], below[s], left[s], right[s]], axis=0))
        for s in range(2)
    ]


def edge_grams(chip, far, near, other):
    return chip[:, K:], far[:, K:], near[:, :, K:], other[:, :, K:]


def second_kernel(sizes, sol_own, sol_other, inter_hbm, gram_hbm, chip_hbm, far_hbm, near_hbm, other_hbm,
                  res_hbm, dir_hbm, fac_hbm, half_hbm,
                  jump0, prod, half, pay,
                  inter, gram, chip, far, near, other, res, dbuf, lbuf, corner, jumpv, prodv, halfv, block, sem):
    copies = Copies(sem)
    edges = (chip, far, near, other)
    loads = [copies.fetch(gram_hbm, gram)]
    loads += [copies.fetch(a, b) for a, b in zip((chip_hbm, far_hbm, near_hbm, other_hbm), edges)]
    loads.append(copies.fetch(inter_hbm, inter))
    res_in = copies.fetch(res_hbm, res)
    dirs = [copies.fetch(dir_hbm.at[s, 0], dbuf.at[s]) for s in range(2)]
    facs = [fetch_lower(copies, fac_hbm.at[s, 0], lbuf.at[s]) for s in range(2)]
    corner_in = copies.fetch(half_hbm.at[:, pl.ds(K, CORN), :], corner)
    for load in loads:
        load.wait()
    jumped = jumps(sizes, sol_own, sol_other, inter, gram, edges, edge_grams(*edges))
    res_in.wait()
    cross = jnp.zeros((1, K), F32)
    energy = jnp.zeros((1, K), F32)
    for s in range(2):
        jumpv[s] = jumped[s]
        copies.send(jumpv.at[s], jump0.at[s])
        cross += jnp.sum(res[s] * jumped[s], axis=0, keepdims=True)
        energy += jnp.sum(jumped[s] * jumped[s], axis=0, keepdims=True)
    for s in range(2):
        dirs[s].wait()
        wide = dot(dbuf[s], jnp.concatenate(split2(jumpv[s]), axis=1))
        prodv[s] = active_mask(sizes[s]) * (wide[:, :K] + wide[:, K:])
        copies.send(prodv.at[s], prod.at[s])
    corner_in.wait()
    corners = []
    for s in range(2):
        left = jnp.concatenate(split2(jnp.transpose(prodv[s])), axis=0)
        wide = times_lower_turned(left, lbuf.at[s], facs[s])
        turned = jnp.concatenate(split2(wide[:K] + wide[K:]), axis=0)
        halfv[s] = turned
        copies.send(halfv.at[s], half.at[s])
        rows = dot_turned(corner[s], turned)
        corners.append(corner_mask(sizes[s]) * (rows[:, :K] + rows[:, K:]))
    rows = [jnp.zeros((1, K), F32)] * 2 + list(split3(cross)) + list(split3(energy))
    send_payload(copies, pay, block, corners, rows_of((16, K), rows))
    copies.finish()


def back_next_kernel(sizes, half_hbm, fac_hbm, inter, chip, far, near, other,
                     half, lbuf, interv, e0, e1, e2, e3, sem):
    copies = Copies(sem)
    facs, halves_in = [], []
    for s in range(2):
        halves_in.append(copies.fetch(half_hbm.at[s], half.at[s]))
        facs.append(fetch_lower(copies, fac_hbm.at[s, 0], lbuf.at[s]))
    for s in range(2):
        halves_in[s].wait()
        for load in facs[s]:
            load.wait()
        wide = times_lower(half.at[s], lbuf.at[s])
        interv[s] = active_mask(sizes[s]) * jnp.transpose(wide[:K] + wide[K:])
        copies.send(interv.at[s], inter.at[s])
    send_edges(copies, (e0, e1, e2, e3), (chip, far, near, other), interv, None)
    copies.finish()


def third_kernel(sizes, sol_own, sol_other, stats, inter_hbm, gram_hbm, chip_hbm, far_hbm, near_hbm, other_hbm,
                 old_chip, old_far, old_near, old_other, res_hbm, jump_hbm,
                 res1, jump1, pay,
                 inter, gram, chip, far, near, other, gchip, gfar, gnear, gother, res, jump0, sem):
    copies = Copies(sem)
    edges = (chip, far, near, other)
    grams = (gchip, gfar, gnear, gother)
    width = pl.ds(K, K)
    loads = [copies.fetch(gram_hbm, gram)]
    loads += [copies.fetch(a.at[:, width], b) for a, b in zip((old_chip, old_far), grams[:2])]
    loads += [copies.fetch(a.at[:, :, width], b) for a, b in zip((old_near, old_other), grams[2:])]
    loads += [copies.fetch(a, b) for a, b in zip((chip_hbm, far_hbm, near_hbm, other_hbm), edges)]
    loads.append(copies.fetch(inter_hbm, inter))
    late = [copies.fetch(res_hbm, res), copies.fetch(jump_hbm, jump0)]
    for load in loads:
        load.wait()
    again = jumps(sizes, sol_own, sol_other, inter, gram, edges, tuple(g[...] for g in grams))
    for load in late:
        load.wait()
    step = stats[0:1] / (stats[1:2] + 1e-06)
    cross = jnp.zeros((1, K), F32)
    energy = jnp.zeros((1, K), F32)
    for s in range(2):
        before = res[s] - step * jump0[s]
        jumped = jump0[s] - step * again[s]
        res1[s] = before
        jump1[s] = jumped
        cross += jnp.sum(before * jumped, axis=0, keepdims=True)
        energy += jnp.sum(jumped * jumped, axis=0, keepdims=True)
    block = rows_of((8, K), [cross, energy])
    for dest in range(CS * YS):
        pay[dest] = block


def partial_kernel(rec, pay):
    total = sum(rec[b] for b in range(CS * YS))
    for dest in range(ZS * XS):
        pay[dest] = total


def last_kernel(rec, stats, res1, jump1, search, prod, mult, res, multv, resv, sem):
    copies = Copies(sem)
    total = sum(rec[b] for b in range(ZS * XS))
    first = stats[0:1] / (stats[1:2] + 1e-06)
    step = total[0:1] / (total[1:2] + 1e-06)
    for s in range(2):
        multv[s] = first * search[s] + step * (search[s] - first * prod[s])
        copies.send(multv.at[s], mult.at[s])
        resv[s] = res1[s] - step * jump1[s]
        copies.send(resv.at[s], res.at[s])
    copies.finish()


def all_to_all(value, axes):
    return lax.all_to_all(value, axes, split_axis=0, concat_axis=0)


def swap(value):
    return lax.ppermute(value, "core", [(0, 1), (1, 0)])


def exchange(chip, far, near, other):
    even = [(i, i ^ 1) for i in range(16)]
    odd = [(i, i + 1) for i in range(1, 15, 2)] + [(i + 1, i) for i in range(1, 15, 2)]
    rows, cols = ("z", "core"), ("x", "y")
    return (
        lax.ppermute(chip, rows, even),
        lax.ppermute(far, rows, odd),
        lax.ppermute(near, cols, even),
        lax.ppermute(other, cols, odd),
    )


def coarse_solution(own, snd, arrived):
    pay3 = ((ZS, HALF + 16, K), BF16)
    rcv = swap(snd)
    (pay,) = call(pair_sum_kernel, [pay3], [VM] * 2, [HB], [(pay3[0][1:], BF16), sems(ZS)])(own, rcv)
    rec = all_to_all(pay, "z")
    pay, stats = call(
        z_sum_kernel,
        [((SY, HALF, K), BF16), ((8, K), F32)],
        [VM, HB, HB],
        [HB, VM],
        [((HALF, K), BF16), sems(SY)],
    )(rec, *arrived[2:])
    sol = all_to_all(pay, ("x", "y"))
    (sol,) = call(tie_kernel, [((SY, HALF, K), BF16)], [AN] + [HB] * 2, [AN], aliases={0: 0})(sol, *arrived[:2])
    sol = sol.reshape(SY * HALF, K)
    return sol, swap(sol), stats


def local(factor, pre, coarse_inv, sizes, cmap, snow_level, pressure):
    sizes = sizes.reshape(2)
    whole = ((2, B, K), F32)
    gramed = ((2, B, K), BF16)
    halved = ((2, 2 * K, B), BF16)
    cornered = ((2, K + CORN, B), BF16)
    square = ((2, B, B), BF16)
    payload = ((SY, ROWS, K), BF16)
    block = (payload[0][1:], BF16)
    sent = [((HALF + 8, K), F32)] * 2

    def edges_of(width):
        return [((E, width), BF16)] * 2 + [((2, E, width), BF16)] * 2

    res, search, half, pay = call(
        first_kernel,
        [whole, whole, cornered, payload],
        [HB] * 6,
        [HB] * 4,
        [square, square, ((2, 1, B, K), BF16), whole, whole, cornered, block]
        + [((2, 1, B), jnp.int32), ((2, 1, CORN), jnp.int32), pltpu.SMEM((2,), jnp.int32), sems(20 + SY)],
    )(sizes, snow_level, cmap, pressure, pre, factor)
    rec = all_to_all(pay, ("x", "y"))
    wide = edges_of(2 * K)
    inter, gram, *edges = call(
        back_first_kernel,
        [whole, gramed] + wide,
        [SM, VM, HB, HB],
        [HB] * 6,
        [cornered, square, whole, gramed] + wide + [sems(18)],
    )(sizes, cmap, half, factor)
    arrived = exchange(*edges)
    own, snd, picked_inv = call(
        coarse_first_kernel,
        sent + [((E, B), BF16)],
        [VM, HB, HB],
        [VM, VM, HB],
        [((E, NC), BF16), ((E, B), BF16), ((NC, B), BF16), sems(2)],
    )(rec, coarse_inv, gram)
    sol_own, sol_other, _ = coarse_solution(own, snd, arrived)
    jump0, prod, half1, pay = call(
        second_kernel,
        [whole, whole, halved, payload],
        [SM, VM, VM] + [HB] * 10,
        [HB] * 4,
        [whole, gramed] + wide + [whole, square, square, ((2, CORN, B), BF16), whole, whole, halved, block, sems(24 + SY)],
    )(sizes, sol_own, sol_other, inter, gram, *arrived, res, pre, factor, half)
    rec = all_to_all(pay, ("x", "y"))
    slim = edges_of(K)
    inter1, *edges = call(
        back_next_kernel,
        [whole] + slim,
        [SM] + [HB] * 2,
        [HB] * 5,
        [halved, square, whole] + slim + [sems(16)],
    )(sizes, half1, factor)
    arrived1 = exchange(*edges)
    own, snd = call(coarse_next_kernel, sent, [VM] * 2 + [HB], [VM] * 2)(rec, picked_inv, inter1)
    sol_own, sol_other, stats = coarse_solution(own, snd, arrived1)
    res1, jump1, pay = call(
        third_kernel,
        [whole] * 2 + [((CS * YS, 8, K), F32)],
        [SM] + [VM] * 3 + [HB] * 12,
        [VM] * 3,
        [whole, gramed] + slim + edges_of(K) + [whole, whole, sems(12)],
    )(sizes, sol_own, sol_other, stats, inter1, gram, *arrived1, *arrived, res, jump0)
    rec = all_to_all(pay, ("core", "y"))
    (pay,) = call(partial_kernel, [((ZS * XS, 8, K), F32)], [VM], [VM])(rec)
    rec = all_to_all(pay, ("z", "x"))
    mult, res = call(last_kernel, [whole] * 2, [VM] * 6, [HB] * 2, [whole, whole, sems(4)])(
        rec, stats, res1, jump1, search, prod
    )
    return mult.reshape(2, 1, B, K), res.reshape(2, 1, B, K)


def solution(mesh):
    fine = Mesh(mesh.devices.reshape(ZS, CS, XS, YS), ("z", "core", "x", "y"))
    rows, cols = ("z", "core"), ("x", "y")
    return jax.shard_map(
        local,
        mesh=fine,
        in_specs=(
            P(rows, cols, None, None),
            P(rows, cols, None, None),
            P(cols, None),
            P(rows, cols),
            P(rows, cols, None),
            P(rows, cols, None),
            P(rows, cols, None, None),
        ),
        out_specs=(P(rows, cols, None, None), P(rows, cols, None, None)),
        check_vma=False,
    )
```

```python
import jax
import jax.numpy as jnp
from jax import lax
from jax.experimental import pallas as pl
from jax.experimental.pallas import tpu as pltpu
from jax.sharding import Mesh
from jax.sharding import PartitionSpec as P

B = 1024
E = 256
K = 128
CORN = 32
NC = 4096
GR = 32
GC = 16
ZS = 8
CS = 2
XS = 4
YS = 4
SY = XS * YS
STRIDE = B // CORN
ROWS = 80
HALF = 128
F32 = jnp.float32
BF16 = jnp.bfloat16
VMEM_LIMIT = 40 * 1024 * 1024

VM = pl.BlockSpec(memory_space=pltpu.VMEM)
SM = pl.BlockSpec(memory_space=pltpu.SMEM)
HB = pl.BlockSpec(memory_space=pltpu.HBM)
AN = pl.BlockSpec(memory_space=pl.ANY)


def dot(a, b):
    return jnp.dot(a, b, preferred_element_type=F32)


def iota(shape, dim):
    return lax.broadcasted_iota(jnp.int32, shape, dim)


def call(kernel, outs, in_specs, out_specs, scratch=(), aliases=None):
    run = pl.pallas_call(
        kernel,
        out_shape=[
            pltpu.HBM(shape, dtype) if spec is HB else jax.ShapeDtypeStruct(shape, dtype)
            for (shape, dtype), spec in zip(outs, out_specs)
        ],
        in_specs=in_specs,
        out_specs=out_specs,
        scratch_shapes=[pltpu.VMEM(*item) if isinstance(item, tuple) else item for item in scratch],
        input_output_aliases=aliases or {},
        compiler_params=pltpu.CompilerParams(vmem_limit_bytes=VMEM_LIMIT),
    )

    def placed(*args):
        return run(
            *[pltpu.with_memory_space_constraint(a, pltpu.HBM) if spec is HB else a for a, spec in zip(args, in_specs)]
        )

    return placed


class Copies:
    def __init__(self, sems):
        self.sems = sems
        self.count = 0
        self.out = []

    def fetch(self, source, target):
        copy = pltpu.make_async_copy(source, target, self.sems.at[self.count])
        self.count += 1
        copy.start()
        return copy

    def send(self, source, target):
        self.out.append(self.fetch(source, target))

    def finish(self):
        for copy in self.out:
            copy.wait()


def sems(count):
    return pltpu.SemaphoreType.DMA((count,))


def fetch_lower(copies, source, target):
    loads = []
    for block in range(B // E):
        rows, cols = pl.ds(block * E, E), pl.ds(0, (block + 1) * E)
        loads.append(copies.fetch(source.at[rows, cols], target.at[rows, cols]))
    return loads


def dot_turned(a, b):
    return lax.dot_general(a, b, (((1,), (1,)), ((), ())), preferred_element_type=F32)


def times_lower_turned(left, matrix, loads):
    for load in loads:
        load.wait()
    parts = []
    for block in range(B // E):
        width = (block + 1) * E
        parts.append(dot_turned(left[:, :width], matrix[block * E : width, :width]))
    return jnp.concatenate(parts, axis=1)


def times_lower(left, matrix):
    parts = []
    for block in range(B // E):
        start = block * E
        parts.append(dot(left[:, start:], matrix[start:, start : start + E]))
    return jnp.concatenate(parts, axis=1)


def split2(value):
    high = value.astype(BF16)
    low = (value - high.astype(F32)).astype(BF16)
    return high, low


def split3(value):
    high, _ = split2(value)
    rest = value - high.astype(F32)
    mid, low = split2(rest)
    return high, mid, low


def active_mask(size):
    return ((iota((B, K), 0) & (E - 1)) < size).astype(F32)


def rows_of(shape, rows):
    index = iota(shape, 0)
    result = jnp.zeros(shape, F32)
    for number, row in enumerate(rows):
        result = jnp.where(index == number, jnp.broadcast_to(row.astype(F32), shape), result)
    return result


def send_payload(copies, pay, block, corners, tail):
    block[...] = jnp.concatenate([c.astype(BF16) for c in corners] + [tail.astype(BF16)], axis=0)
    for dest in range(SY):
        copies.send(block, pay.at[dest])


def send_edges(copies, bufs, targets, interface, extra):
    chip, far, near, other = bufs
    core = lax.axis_index("core")
    odd = lax.axis_index("y") & 1

    def packed(s, edge):
        rows = pl.ds(pl.multiple_of(edge * E, E), E)
        parts = [interface[s, rows, :].astype(BF16)]
        if extra is not None:
            parts.append(extra[s, rows, :])
        return jnp.concatenate(parts, axis=1)

    chip[...] = packed(1 - core, 1 - core)
    far[...] = packed(core, core)
    for s in range(2):
        near[s] = packed(s, 3 - odd)
        other[s] = packed(s, 2 + odd)
    for source, target in zip(bufs, targets):
        copies.send(source, target)


def first_kernel(sizes_hbm, snow_hbm, cmap_hbm, press_hbm, dir_hbm, fac_hbm,
                 res, search, half, pay, dbuf, lbuf, press, resv, searchv, halfv, block, snow, cmap, sizes, sem):
    copies = Copies(sem)
    small = [copies.fetch(a, b) for a, b in ((sizes_hbm, sizes), (snow_hbm, snow), (cmap_hbm, cmap))]
    load = copies.fetch(press_hbm, press)
    dirs, facs = [], []
    for s in range(2):
        dirs.append(copies.fetch(dir_hbm.at[s, 0], dbuf.at[s]))
    for s in range(2):
        facs.append(fetch_lower(copies, fac_hbm.at[s, 0], lbuf.at[s]))
    grid_row = lax.axis_index("z") * (2 * CS) + lax.axis_index("core") * 2
    grid_col = lax.axis_index("x") * YS + lax.axis_index("y")
    for copy in small:
        copy.wait()
    masks = [active_mask(sizes[s]) for s in range(2)]
    pick = jnp.where(iota((CORN, B), 1) == iota((CORN, B), 0) * STRIDE, 1.0, 0.0).astype(BF16)
    columns = []
    for s in range(2):
        place = jnp.full((1, B), grid_row + s + grid_col, jnp.int32).astype(F32)
        drift = 1.0 + 2.0 * place / (GR + GC - 2)
        depth = 0.5 + 0.25 * snow[s].astype(F32)
        present = (iota((1, B), 1) & (E - 1)) < sizes[s]
        scale = jnp.where(present, depth * drift, 0.0)
        columns.append(jnp.transpose(jnp.broadcast_to(scale, (K, B))))
    load.wait()
    for s in range(2):
        resv[s] = press[s, 0].astype(F32) * columns[s]
        copies.send(resv.at[s], res.at[s])
    for s in range(2):
        dirs[s].wait()
        searchv[s] = masks[s] * dot(dbuf[s], resv[s].astype(BF16))
        copies.send(searchv.at[s], search.at[s])
    corners = []
    for s in range(2):
        left = jnp.concatenate([jnp.transpose(searchv[s]).astype(BF16), pick], axis=0)
        turned = times_lower_turned(left, lbuf.at[s], facs[s]).astype(BF16)
        halfv[s] = turned
        copies.send(halfv.at[s], half.at[s])
        rows = dot_turned(turned[K:], turned[:K])
        corners.append(corner_mask(sizes[s]) * rows)
    cm = two_rows(cmap)
    tail = rows_of((16, K), [(cm >> 8).astype(F32), (cm & 255).astype(F32)])
    send_payload(copies, pay, block, corners, tail)
    copies.finish()


def corner_mask(size):
    return (((iota((CORN, K), 0) * STRIDE) & (E - 1)) < size).astype(F32)


def tiled_row(row):
    return jnp.concatenate([row] * (K // CORN), axis=1)


def two_rows(cmap):
    lane = iota((1, K), 1)
    return jnp.where((lane & CORN) == 0, tiled_row(cmap[0]), tiled_row(cmap[1]))


def back_first_kernel(sizes, cmap, half_hbm, fac_hbm, inter, gram, chip, far, near, other,
                      half, lbuf, interv, gramv, e0, e1, e2, e3, sem):
    copies = Copies(sem)
    facs, halves_in = [], []
    for s in range(2):
        halves_in.append(copies.fetch(half_hbm.at[s], half.at[s]))
        facs.append(fetch_lower(copies, fac_hbm.at[s, 0], lbuf.at[s]))
    lane = iota((B, K), 1)
    for s in range(2):
        mask = active_mask(sizes[s])
        square = jnp.transpose(jnp.broadcast_to(tiled_row(cmap[s]), (K, K)))
        column = jnp.concatenate([square] * (B // K), axis=0)
        digits = jnp.where(lane < 96, column >> 8, column & 255).astype(F32)
        halves_in[s].wait()
        for load in facs[s]:
            load.wait()
        back = jnp.transpose(times_lower(half.at[s], lbuf.at[s]))
        interv[s] = mask * back[:, :K]
        copies.send(interv.at[s], inter.at[s])
        ghigh, glow = split2(mask * jnp.concatenate([back[:, K:], jnp.zeros((B, K - CORN), F32)], axis=1))
        low_moved = pltpu.roll(glow.astype(F32), CORN, axis=1)
        gramv[s] = jnp.where(
            lane < CORN, ghigh.astype(F32), jnp.where(lane < 2 * CORN, low_moved, digits)
        ).astype(BF16)
        copies.send(gramv.at[s], gram.at[s])
    send_edges(copies, (e0, e1, e2, e3), (chip, far, near, other), interv, gramv)
    copies.finish()


def coarse_rows(rec):
    return jnp.concatenate([rec[b, 0:64, :] for b in range(SY)], axis=0)


def halves(value, stats, own, snd):
    mine = lax.axis_index("core") == 0
    tail = rows_of((8, K), stats)
    own[0:HALF] = jnp.where(mine, value[:HALF], value[HALF:])
    snd[0:HALF] = jnp.where(mine, value[HALF:], value[:HALF])
    own[HALF : HALF + 8] = tail
    snd[HALF : HALF + 8] = tail


def coarse_first_kernel(rec, coarse_hbm, _, own, snd, picked_inv, coarse, matrix, hot, sem):
    copies = Copies(sem)
    load = copies.fetch(coarse_hbm, coarse)
    lane = iota((1, K), 1)
    tails = [rec[b, 64:80, :].astype(F32) for b in range(SY)]

    def row(number):
        parts = [
            jnp.where(lane < 64, tails[2 * m][number : number + 1], tails[2 * m + 1][number : number + 1])
            for m in range(SY // 2)
        ]
        return jnp.concatenate(parts, axis=1)

    high, low = row(0), row(1)
    low_hot = jnp.where(iota((E, B), 0) == low.astype(jnp.int32), 1.0, 0.0).astype(BF16)
    high_hot = jnp.where(iota((NC // E, B), 0) == high.astype(jnp.int32), 1.0, 0.0).astype(BF16)
    for digit in range(NC // E):
        hot[digit * E : (digit + 1) * E] = low_hot * high_hot[digit : digit + 1]
    load.wait()
    matrix[...] = dot(coarse[...], hot[...]).astype(BF16)
    copies.send(matrix, picked_inv)
    halves(dot(matrix[...], coarse_rows(rec)), [], own, snd)
    copies.finish()


def coarse_next_kernel(rec, picked_inv, _, own, snd):
    value = dot(picked_inv[...], coarse_rows(rec))
    tails = sum(rec[b, 64:80, :].astype(F32) for b in range(SY))
    stats = [tails[q : q + 1] + tails[q + 1 : q + 2] + tails[q + 2 : q + 3] for q in (2, 5)]
    halves(value, stats, own, snd)


def pair_sum_kernel(own, rcv, pay, block, sem):
    copies = Copies(sem)
    total = own[...] + rcv[...]
    rows = []
    for q in range(2):
        rows += list(split3(total[HALF + q : HALF + q + 1]))
    tail = rows_of((16, K), rows).astype(BF16)
    block[...] = jnp.concatenate([total[:HALF].astype(BF16), tail], axis=0)
    for dest in range(ZS):
        copies.send(block, pay.at[dest])
    copies.finish()


def z_sum_kernel(rec, _, __, pay, stats, block, sem):
    copies = Copies(sem)
    total = sum(rec[z].astype(F32) for z in range(ZS))
    block[...] = total[:HALF].astype(BF16)
    for dest in range(SY):
        copies.send(block, pay.at[dest])
    rows = total[HALF:]
    stats[...] = rows_of(
        (8, K), [rows[q : q + 1] + rows[q + 1 : q + 2] + rows[q + 2 : q + 3] for q in (0, 3)]
    )
    copies.finish()


def preload_kernel(_, *refs):
    count = len(refs) // 2
    copies = Copies(refs[-1])
    for source, target in zip(refs[:count], refs[count:-1]):
        copies.send(source, target)
    copies.finish()


def tie_kernel(source, _, __, target):
    pass


def jumps(sizes, sol_own, sol_other, inter, gram, edges, grams):
    core = lax.axis_index("core")
    odd = lax.axis_index("y") & 1
    chip, far, near, other = edges
    gchip, gfar, gnear, gother = grams

    def ordered(flag, a, b):
        return jnp.where(flag == 0, b, a), jnp.where(flag == 0, a, b)

    north, south = ordered(core, chip[...], far[...])
    gnorth, gsouth = ordered(core, gchip, gfar)
    west, east = ordered(odd, near[...], other[...])
    gwest, geast = ordered(odd, gnear, gother)
    gram_edges = [gram[0, 0:CORN, :], gram[1, 0:CORN, :], gnorth[0:CORN], gsouth[0:CORN]]
    gram_edges += [g[s, 0:CORN, :] for g in (gwest, geast) for s in range(2)]
    digits = jnp.concatenate(gram_edges, axis=0).astype(F32)
    cm = digits[:, 64:65].astype(jnp.int32) * 256 + digits[:, 96:97].astype(jnp.int32)
    half = ((cm >> 7) & 1) ^ core
    place = half * 2048 + (cm >> 8) * HALF + (cm & (HALF - 1))
    hot = jnp.where(iota((8 * CORN, NC), 1) == place, 1.0, 0.0).astype(BF16)
    picks = (dot(hot[:, :2048], sol_own[...]) + dot(hot[:, 2048:], sol_other[...])).astype(BF16)
    zero = jnp.zeros((2 * CORN, K), BF16)

    def stacked(number):
        rows = picks[number * CORN : (number + 1) * CORN]
        return jnp.concatenate([rows, rows, zero], axis=0)

    full = [inter[s] + dot(gram[s], stacked(s)) for s in range(2)]

    def arrived(edge, gedge, number):
        return edge[:, :K].astype(F32) + dot(gedge, stacked(number))

    above = [arrived(north, gnorth, 2), full[0][E : 2 * E]]
    below = [full[1][0:E], arrived(south, gsouth, 3)]
    left = [arrived(west[s], gwest[s], 4 + s) for s in range(2)]
    right = [arrived(east[s], geast[s], 6 + s) for s in range(2)]
    return [
        active_mask(sizes[s]) * (full[s] - jnp.concatenate([above[s], below[s], left[s], right[s]], axis=0))
        for s in range(2)
    ]


def edge_grams(chip, far, near, other):
    return chip[:, K:], far[:, K:], near[:, :, K:], other[:, :, K:]


def second_kernel(sizes, sol_own, sol_other, inter, gram, chip, far, near, other,
                  res_hbm, dir_hbm, fac_hbm, half_hbm,
                  jump0, prod, half, pay,
                  res, dbuf, lbuf, corner, jumpv, prodv, halfv, block, sem):
    copies = Copies(sem)
    edges = (chip, far, near, other)
    dirs = [copies.fetch(dir_hbm.at[s, 0], dbuf.at[s]) for s in range(2)]
    facs = [fetch_lower(copies, fac_hbm.at[s, 0], lbuf.at[s]) for s in range(2)]
    corner_in = copies.fetch(half_hbm.at[:, pl.ds(K, CORN), :], corner)
    res_in = copies.fetch(res_hbm, res)
    jumped = jumps(sizes, sol_own, sol_other, inter, gram, edges, edge_grams(*edges))
    for s in range(2):
        jumpv[s] = jumped[s]
        copies.send(jumpv.at[s], jump0.at[s])
    for s in range(2):
        dirs[s].wait()
        prodv[s] = active_mask(sizes[s]) * dot(dbuf[s], jumpv[s].astype(BF16))
        copies.send(prodv.at[s], prod.at[s])
    corner_in.wait()
    corners = []
    for s in range(2):
        turned = times_lower_turned(jnp.transpose(prodv[s]).astype(BF16), lbuf.at[s], facs[s]).astype(BF16)
        halfv[s] = turned
        copies.send(halfv.at[s], half.at[s])
        corners.append(corner_mask(sizes[s]) * dot_turned(corner[s], turned))
    res_in.wait()
    cross = sum(jnp.sum(res[s] * jumpv[s], axis=0, keepdims=True) for s in range(2))
    energy = sum(jnp.sum(jumpv[s] * jumpv[s], axis=0, keepdims=True) for s in range(2))
    rows = [jnp.zeros((1, K), F32)] * 2 + list(split3(cross)) + list(split3(energy))
    send_payload(copies, pay, block, corners, rows_of((16, K), rows))
    copies.finish()


def back_next_kernel(sizes, half_hbm, fac_hbm, inter, chip, far, near, other,
                     half, lbuf, interv, e0, e1, e2, e3, sem):
    copies = Copies(sem)
    facs, halves_in = [], []
    for s in range(2):
        halves_in.append(copies.fetch(half_hbm.at[s], half.at[s]))
        facs.append(fetch_lower(copies, fac_hbm.at[s, 0], lbuf.at[s]))
    for s in range(2):
        halves_in[s].wait()
        for load in facs[s]:
            load.wait()
        interv[s] = active_mask(sizes[s]) * jnp.transpose(times_lower(half.at[s], lbuf.at[s]))
        copies.send(interv.at[s], inter.at[s])
    send_edges(copies, (e0, e1, e2, e3), (chip, far, near, other), interv, None)
    copies.finish()


def third_kernel(sizes, sol_own, sol_other, stats, inter, gram, chip, far, near, other,
                 old_chip, old_far, old_near, old_other, res_hbm, jump_hbm,
                 res1, jump1, pay, res, jump0, sem):
    copies = Copies(sem)
    edges = (chip, far, near, other)
    late = [copies.fetch(res_hbm, res), copies.fetch(jump_hbm, jump0)]
    grams = edge_grams(old_chip, old_far, old_near, old_other)
    again = jumps(sizes, sol_own, sol_other, inter, gram, edges, grams)
    for load in late:
        load.wait()
    step = stats[0:1] / (stats[1:2] + 1e-06)
    cross = jnp.zeros((1, K), F32)
    energy = jnp.zeros((1, K), F32)
    for s in range(2):
        before = res[s] - step * jump0[s]
        jumped = jump0[s] - step * again[s]
        res1[s] = before
        jump1[s] = jumped
        cross += jnp.sum(before * jumped, axis=0, keepdims=True)
        energy += jnp.sum(jumped * jumped, axis=0, keepdims=True)
    block = rows_of((8, K), [cross, energy])
    for dest in range(CS * YS):
        pay[dest] = block


def partial_kernel(rec, pay):
    total = sum(rec[b] for b in range(CS * YS))
    for dest in range(ZS * XS):
        pay[dest] = total


def last_kernel(rec, stats, res1, jump1, search, prod, mult, res, multv, resv, sem):
    copies = Copies(sem)
    total = sum(rec[b] for b in range(ZS * XS))
    first = stats[0:1] / (stats[1:2] + 1e-06)
    step = total[0:1] / (total[1:2] + 1e-06)
    for s in range(2):
        multv[s] = first * search[s] + step * (search[s] - first * prod[s])
        copies.send(multv.at[s], mult.at[s])
        resv[s] = res1[s] - step * jump1[s]
        copies.send(resv.at[s], res.at[s])
    copies.finish()


def all_to_all(value, axes):
    return lax.all_to_all(value, axes, split_axis=0, concat_axis=0)


def swap(value):
    return lax.ppermute(value, "core", [(0, 1), (1, 0)])


def exchange(chip, far, near, other):
    even = [(i, i ^ 1) for i in range(16)]
    odd = [(i, i + 1) for i in range(1, 15, 2)] + [(i + 1, i) for i in range(1, 15, 2)]
    rows, cols = ("z", "core"), ("x", "y")
    return (
        lax.ppermute(chip, rows, even),
        lax.ppermute(far, rows, odd),
        lax.ppermute(near, cols, even),
        lax.ppermute(other, cols, odd),
    )


def coarse_solution(own, snd, arrived, needed):
    pay3 = ((ZS, HALF + 16, K), BF16)
    rcv = swap(snd)
    (pay,) = call(pair_sum_kernel, [pay3], [VM] * 2, [HB], [(pay3[0][1:], BF16), sems(ZS)])(own, rcv)
    rec = all_to_all(pay, "z")
    pay, stats = call(
        z_sum_kernel,
        [((SY, HALF, K), BF16), ((8, K), F32)],
        [VM, HB, HB],
        [HB, VM],
        [((HALF, K), BF16), sems(SY)],
    )(rec, *arrived[2:])
    sol = all_to_all(pay, ("x", "y"))
    (sol,) = call(tie_kernel, [((SY, HALF, K), BF16)], [AN] + [HB] * 2, [AN], aliases={0: 0})(sol, *arrived[:2])
    kinds = [(a.shape, a.dtype) for a in needed]
    needed = call(preload_kernel, kinds, [AN] + [HB] * len(kinds), [VM] * len(kinds), [sems(len(kinds))])(sol, *needed)
    sol = sol.reshape(SY * HALF, K)
    return sol, swap(sol), stats, needed


def local(factor, pre, coarse_inv, sizes, cmap, snow_level, pressure):
    sizes = sizes.reshape(2)
    whole = ((2, B, K), F32)
    gramed = ((2, B, K), BF16)
    halved = ((2, K, B), BF16)
    cornered = ((2, K + CORN, B), BF16)
    square = ((2, B, B), BF16)
    payload = ((SY, ROWS, K), BF16)
    block = (payload[0][1:], BF16)
    sent = [((HALF + 8, K), F32)] * 2

    def edges_of(width):
        return [((E, width), BF16)] * 2 + [((2, E, width), BF16)] * 2

    res, search, half, pay = call(
        first_kernel,
        [whole, whole, cornered, payload],
        [HB] * 6,
        [HB] * 4,
        [square, square, ((2, 1, B, K), BF16), whole, whole, cornered, block]
        + [((2, 1, B), jnp.int32), ((2, 1, CORN), jnp.int32), pltpu.SMEM((2,), jnp.int32), sems(20 + SY)],
    )(sizes, snow_level, cmap, pressure, pre, factor)
    rec = all_to_all(pay, ("x", "y"))
    wide = edges_of(2 * K)
    inter, gram, *edges = call(
        back_first_kernel,
        [whole, gramed] + wide,
        [SM, VM, HB, HB],
        [HB] * 6,
        [cornered, square, whole, gramed] + wide + [sems(18)],
    )(sizes, cmap, half, factor)
    arrived = exchange(*edges)
    own, snd, picked_inv = call(
        coarse_first_kernel,
        sent + [((E, B), BF16)],
        [VM, HB, HB],
        [VM, VM, HB],
        [((E, NC), BF16), ((E, B), BF16), ((NC, B), BF16), sems(2)],
    )(rec, coarse_inv, gram)
    sol_own, sol_other, _, needed = coarse_solution(own, snd, arrived, [inter, gram, *arrived])
    jump0, prod, half1, pay = call(
        second_kernel,
        [whole, whole, halved, payload],
        [SM] + [VM] * 8 + [HB] * 4,
        [HB] * 4,
        [whole, square, square, ((2, CORN, B), BF16), whole, whole, halved, block, sems(24 + SY)],
    )(sizes, sol_own, sol_other, *needed, res, pre, factor, half)
    rec = all_to_all(pay, ("x", "y"))
    slim = edges_of(K)
    inter1, *edges = call(
        back_next_kernel,
        [whole] + slim,
        [SM] + [HB] * 2,
        [HB] * 5,
        [halved, square, whole] + slim + [sems(16)],
    )(sizes, half1, factor)
    arrived1 = exchange(*edges)
    own, snd = call(coarse_next_kernel, sent, [VM] * 2 + [HB], [VM] * 2)(rec, picked_inv, inter1)
    sol_own, sol_other, stats, needed = coarse_solution(own, snd, arrived1, [inter1, gram, *arrived1, *arrived])
    res1, jump1, pay = call(
        third_kernel,
        [whole] * 2 + [((CS * YS, 8, K), F32)],
        [SM] + [VM] * 13 + [HB] * 2,
        [VM] * 3,
        [whole, whole, sems(2)],
    )(sizes, sol_own, sol_other, stats, *needed, res, jump0)
    rec = all_to_all(pay, ("core", "y"))
    (pay,) = call(partial_kernel, [((ZS * XS, 8, K), F32)], [VM], [VM])(rec)
    rec = all_to_all(pay, ("z", "x"))
    mult, res = call(last_kernel, [whole] * 2, [VM] * 6, [HB] * 2, [whole, whole, sems(4)])(
        rec, stats, res1, jump1, search, prod
    )
    return mult.reshape(2, 1, B, K), res.reshape(2, 1, B, K)


def solution(mesh):
    fine = Mesh(mesh.devices.reshape(ZS, CS, XS, YS), ("z", "core", "x", "y"))
    rows, cols = ("z", "core"), ("x", "y")
    return jax.shard_map(
        local,
        mesh=fine,
        in_specs=(
            P(rows, cols, None, None),
            P(rows, cols, None, None),
            P(cols, None),
            P(rows, cols),
            P(rows, cols, None),
            P(rows, cols, None),
            P(rows, cols, None, None),
        ),
        out_specs=(P(rows, cols, None, None), P(rows, cols, None, None)),
        check_vma=False,
    )
```

```python
import jax
import jax.numpy as jnp
from jax import lax
from jax.experimental import pallas as pl
from jax.experimental.pallas import tpu as pltpu
from jax.sharding import Mesh
from jax.sharding import PartitionSpec as P

B = 1024
E = 256
K = 128
CORN = 32
NC = 4096
GR = 32
GC = 16
ZS = 8
CS = 2
XS = 4
YS = 4
SY = XS * YS
STRIDE = B // CORN
ROWS = 80
HALF = 128
F32 = jnp.float32
BF16 = jnp.bfloat16
VMEM_LIMIT = 40 * 1024 * 1024

VM = pl.BlockSpec(memory_space=pltpu.VMEM)
SM = pl.BlockSpec(memory_space=pltpu.SMEM)
HB = pl.BlockSpec(memory_space=pltpu.HBM)
AN = pl.BlockSpec(memory_space=pl.ANY)


def dot(a, b):
    return jnp.dot(a, b, preferred_element_type=F32)


def iota(shape, dim):
    return lax.broadcasted_iota(jnp.int32, shape, dim)


def call(kernel, outs, in_specs, out_specs, scratch=(), aliases=None):
    run = pl.pallas_call(
        kernel,
        out_shape=[
            pltpu.HBM(shape, dtype) if spec is HB else jax.ShapeDtypeStruct(shape, dtype)
            for (shape, dtype), spec in zip(outs, out_specs)
        ],
        in_specs=in_specs,
        out_specs=out_specs,
        scratch_shapes=[pltpu.VMEM(*item) if isinstance(item, tuple) else item for item in scratch],
        input_output_aliases=aliases or {},
        compiler_params=pltpu.CompilerParams(vmem_limit_bytes=VMEM_LIMIT),
    )

    def placed(*args):
        return run(
            *[pltpu.with_memory_space_constraint(a, pltpu.HBM) if spec is HB else a for a, spec in zip(args, in_specs)]
        )

    return placed


class Copies:
    def __init__(self, sems):
        self.sems = sems
        self.count = 0
        self.out = []

    def fetch(self, source, target):
        copy = pltpu.make_async_copy(source, target, self.sems.at[self.count])
        self.count += 1
        copy.start()
        return copy

    def send(self, source, target):
        self.out.append(self.fetch(source, target))

    def finish(self):
        for copy in self.out:
            copy.wait()


def sems(count):
    return pltpu.SemaphoreType.DMA((count,))


def fetch_lower(copies, source, target):
    loads = []
    for block in range(B // E):
        rows, cols = pl.ds(block * E, E), pl.ds(0, (block + 1) * E)
        loads.append(copies.fetch(source.at[rows, cols], target.at[rows, cols]))
    return loads


def dot_turned(a, b):
    return lax.dot_general(a, b, (((1,), (1,)), ((), ())), preferred_element_type=F32)


def times_lower_turned(left, matrix, loads):
    for load in loads:
        load.wait()
    parts = []
    for block in range(B // E):
        width = (block + 1) * E
        parts.append(dot_turned(left[:, :width], matrix[block * E : width, :width]))
    return jnp.concatenate(parts, axis=1)


def times_lower(left, matrix):
    parts = []
    for block in range(B // E):
        start = block * E
        parts.append(dot(left[:, start:], matrix[start:, start : start + E]))
    return jnp.concatenate(parts, axis=1)


def split2(value):
    high = value.astype(BF16)
    low = (value - high.astype(F32)).astype(BF16)
    return high, low


def split3(value):
    high, _ = split2(value)
    rest = value - high.astype(F32)
    mid, low = split2(rest)
    return high, mid, low


def active_mask(size):
    return ((iota((B, K), 0) & (E - 1)) < size).astype(F32)


def rows_of(shape, rows):
    index = iota(shape, 0)
    result = jnp.zeros(shape, F32)
    for number, row in enumerate(rows):
        result = jnp.where(index == number, jnp.broadcast_to(row.astype(F32), shape), result)
    return result


def send_payload(copies, pay, block, corners, tail):
    block[...] = jnp.concatenate([c.astype(BF16) for c in corners] + [tail.astype(BF16)], axis=0)
    for dest in range(SY):
        copies.send(block, pay.at[dest])


def send_edges(copies, bufs, targets, interface, extra):
    chip, far, near, other = bufs
    core = lax.axis_index("core")
    odd = lax.axis_index("y") & 1

    def packed(s, edge):
        rows = pl.ds(pl.multiple_of(edge * E, E), E)
        parts = [interface[s, rows, :].astype(BF16)]
        if extra is not None:
            parts.append(extra[s, rows, :])
        return jnp.concatenate(parts, axis=1)

    chip[...] = packed(1 - core, 1 - core)
    far[...] = packed(core, core)
    for s in range(2):
        near[s] = packed(s, 3 - odd)
        other[s] = packed(s, 2 + odd)
    for source, target in zip(bufs, targets):
        copies.send(source, target)


def first_kernel(sizes_hbm, snow_hbm, cmap_hbm, press_hbm, dir_hbm, fac_hbm,
                 res, search, half, pay, dbuf, lbuf, press, resv, searchv, halfv, block, snow, cmap, sizes, sem):
    copies = Copies(sem)
    small = [copies.fetch(a, b) for a, b in ((sizes_hbm, sizes), (snow_hbm, snow), (cmap_hbm, cmap))]
    load = copies.fetch(press_hbm, press)
    dirs, facs = [], []
    for s in range(2):
        dirs.append(copies.fetch(dir_hbm.at[s, 0], dbuf.at[s]))
    for s in range(2):
        facs.append(fetch_lower(copies, fac_hbm.at[s, 0], lbuf.at[s]))
    grid_row = lax.axis_index("z") * (2 * CS) + lax.axis_index("core") * 2
    grid_col = lax.axis_index("x") * YS + lax.axis_index("y")
    for copy in small:
        copy.wait()
    masks = [active_mask(sizes[s]) for s in range(2)]
    pick = jnp.where(iota((CORN, B), 1) == iota((CORN, B), 0) * STRIDE, 1.0, 0.0).astype(BF16)
    columns = []
    for s in range(2):
        place = jnp.full((1, B), grid_row + s + grid_col, jnp.int32).astype(F32)
        drift = 1.0 + 2.0 * place / (GR + GC - 2)
        depth = 0.5 + 0.25 * snow[s].astype(F32)
        present = (iota((1, B), 1) & (E - 1)) < sizes[s]
        scale = jnp.where(present, depth * drift, 0.0)
        columns.append(jnp.transpose(jnp.broadcast_to(scale, (K, B))))
    load.wait()
    for s in range(2):
        resv[s] = press[s, 0].astype(F32) * columns[s]
        copies.send(resv.at[s], res.at[s])
    for s in range(2):
        dirs[s].wait()
        searchv[s] = masks[s] * dot(dbuf[s], resv[s].astype(BF16))
        copies.send(searchv.at[s], search.at[s])
    corners = []
    for s in range(2):
        left = jnp.concatenate([jnp.transpose(searchv[s]).astype(BF16), pick], axis=0)
        turned = times_lower_turned(left, lbuf.at[s], facs[s]).astype(BF16)
        halfv[s] = turned
        copies.send(halfv.at[s], half.at[s])
        rows = dot_turned(turned[K:], turned[:K])
        corners.append(corner_mask(sizes[s]) * rows)
    cm = two_rows(cmap)
    tail = rows_of((16, K), [(cm >> 8).astype(F32), (cm & 255).astype(F32)])
    send_payload(copies, pay, block, corners, tail)
    copies.finish()


def corner_mask(size):
    return (((iota((CORN, K), 0) * STRIDE) & (E - 1)) < size).astype(F32)


def tiled_row(row):
    return jnp.concatenate([row] * (K // CORN), axis=1)


def two_rows(cmap):
    lane = iota((1, K), 1)
    return jnp.where((lane & CORN) == 0, tiled_row(cmap[0]), tiled_row(cmap[1]))


def back_first_kernel(sizes, cmap, half_hbm, fac_hbm, inter, gram, chip, far, near, other,
                      half, lbuf, interv, gramv, e0, e1, e2, e3, sem):
    copies = Copies(sem)
    facs, halves_in = [], []
    for s in range(2):
        halves_in.append(copies.fetch(half_hbm.at[s], half.at[s]))
        facs.append(fetch_lower(copies, fac_hbm.at[s, 0], lbuf.at[s]))
    lane = iota((B, K), 1)
    for s in range(2):
        mask = active_mask(sizes[s])
        square = jnp.transpose(jnp.broadcast_to(tiled_row(cmap[s]), (K, K)))
        column = jnp.concatenate([square] * (B // K), axis=0)
        digits = jnp.where(lane < 96, column >> 8, column & 255).astype(F32)
        halves_in[s].wait()
        for load in facs[s]:
            load.wait()
        back = jnp.transpose(times_lower(half.at[s], lbuf.at[s]))
        interv[s] = mask * back[:, :K]
        copies.send(interv.at[s], inter.at[s])
        ghigh, glow = split2(mask * jnp.concatenate([back[:, K:], jnp.zeros((B, K - CORN), F32)], axis=1))
        low_moved = pltpu.roll(glow.astype(F32), CORN, axis=1)
        gramv[s] = jnp.where(
            lane < CORN, ghigh.astype(F32), jnp.where(lane < 2 * CORN, low_moved, digits)
        ).astype(BF16)
        copies.send(gramv.at[s], gram.at[s])
    send_edges(copies, (e0, e1, e2, e3), (chip, far, near, other), interv, gramv)
    copies.finish()


def coarse_rows(rec):
    return jnp.concatenate([rec[b, 0:64, :] for b in range(SY)], axis=0)


def halves(value, stats, own, snd):
    mine = lax.axis_index("core") == 0
    tail = rows_of((8, K), stats)
    own[0:HALF] = jnp.where(mine, value[:HALF], value[HALF:])
    snd[0:HALF] = jnp.where(mine, value[HALF:], value[:HALF])
    own[HALF : HALF + 8] = tail
    snd[HALF : HALF + 8] = tail


def coarse_first_kernel(rec, coarse_hbm, _, own, snd, picked_inv, coarse, matrix, hot, sem):
    copies = Copies(sem)
    load = copies.fetch(coarse_hbm, coarse)
    lane = iota((1, K), 1)
    tails = [rec[b, 64:80, :].astype(F32) for b in range(SY)]

    def row(number):
        parts = [
            jnp.where(lane < 64, tails[2 * m][number : number + 1], tails[2 * m + 1][number : number + 1])
            for m in range(SY // 2)
        ]
        return jnp.concatenate(parts, axis=1)

    high, low = row(0), row(1)
    low_hot = jnp.where(iota((E, B), 0) == low.astype(jnp.int32), 1.0, 0.0).astype(BF16)
    high_hot = jnp.where(iota((NC // E, B), 0) == high.astype(jnp.int32), 1.0, 0.0).astype(BF16)
    for digit in range(NC // E):
        hot[digit * E : (digit + 1) * E] = low_hot * high_hot[digit : digit + 1]
    load.wait()
    matrix[...] = dot(coarse[...], hot[...]).astype(BF16)
    copies.send(matrix, picked_inv)
    halves(dot(matrix[...], coarse_rows(rec)), [], own, snd)
    copies.finish()


def coarse_next_kernel(rec, picked_inv, _, own, snd):
    value = dot(picked_inv[...], coarse_rows(rec))
    tails = sum(rec[b, 64:80, :].astype(F32) for b in range(SY))
    stats = [tails[q : q + 1] + tails[q + 1 : q + 2] + tails[q + 2 : q + 3] for q in (2, 5)]
    halves(value, stats, own, snd)


def pair_sum_kernel(own, rcv, pay, block, sem):
    copies = Copies(sem)
    total = own[...] + rcv[...]
    rows = []
    for q in range(2):
        rows += list(split3(total[HALF + q : HALF + q + 1]))
    tail = rows_of((16, K), rows).astype(BF16)
    block[...] = jnp.concatenate([total[:HALF].astype(BF16), tail], axis=0)
    for dest in range(ZS):
        copies.send(block, pay.at[dest])
    copies.finish()


def z_sum_kernel(rec, _, __, pay, stats, block, sem):
    copies = Copies(sem)
    total = sum(rec[z].astype(F32) for z in range(ZS))
    block[...] = total[:HALF].astype(BF16)
    for dest in range(SY):
        copies.send(block, pay.at[dest])
    rows = total[HALF:]
    stats[...] = rows_of(
        (8, K), [rows[q : q + 1] + rows[q + 1 : q + 2] + rows[q + 2 : q + 3] for q in (0, 3)]
    )
    copies.finish()


def preload_kernel(_, *refs):
    count = len(refs) // 2
    copies = Copies(refs[-1])
    for source, target in zip(refs[:count], refs[count:-1]):
        copies.send(source, target)
    copies.finish()


def tie_kernel(source, _, __, target):
    pass


def jumps(sizes, sol_own, sol_other, inter, gram, edges, grams):
    core = lax.axis_index("core")
    odd = lax.axis_index("y") & 1
    chip, far, near, other = edges
    gchip, gfar, gnear, gother = grams

    def ordered(flag, a, b):
        return jnp.where(flag == 0, b, a), jnp.where(flag == 0, a, b)

    north, south = ordered(core, chip[...], far[...])
    gnorth, gsouth = ordered(core, gchip, gfar)
    west, east = ordered(odd, near[...], other[...])
    gwest, geast = ordered(odd, gnear, gother)
    gram_edges = [gram[0, 0:CORN, :], gram[1, 0:CORN, :], gnorth[0:CORN], gsouth[0:CORN]]
    gram_edges += [g[s, 0:CORN, :] for g in (gwest, geast) for s in range(2)]
    digits = jnp.concatenate(gram_edges, axis=0).astype(F32)
    cm = digits[:, 64:65].astype(jnp.int32) * 256 + digits[:, 96:97].astype(jnp.int32)
    half = ((cm >> 7) & 1) ^ core
    place = half * 2048 + (cm >> 8) * HALF + (cm & (HALF - 1))
    hot = jnp.where(iota((8 * CORN, NC), 1) == place, 1.0, 0.0).astype(BF16)
    picks = (dot(hot[:, :2048], sol_own[...]) + dot(hot[:, 2048:], sol_other[...])).astype(BF16)
    zero = jnp.zeros((2 * CORN, K), BF16)

    def stacked(number):
        rows = picks[number * CORN : (number + 1) * CORN]
        return jnp.concatenate([rows, rows, zero], axis=0)

    full = [inter[s] + dot(gram[s], stacked(s)) for s in range(2)]

    def arrived(edge, gedge, number):
        return edge[:, :K].astype(F32) + dot(gedge, stacked(number))

    above = [arrived(north, gnorth, 2), full[0][E : 2 * E]]
    below = [full[1][0:E], arrived(south, gsouth, 3)]
    left = [arrived(west[s], gwest[s], 4 + s) for s in range(2)]
    right = [arrived(east[s], geast[s], 6 + s) for s in range(2)]
    return [
        active_mask(sizes[s]) * (full[s] - jnp.concatenate([above[s], below[s], left[s], right[s]], axis=0))
        for s in range(2)
    ]


def edge_grams(chip, far, near, other):
    return chip[:, K:], far[:, K:], near[:, :, K:], other[:, :, K:]


def second_kernel(sizes, sol_own, sol_other, inter, gram, chip, far, near, other,
                  res_hbm, dir_hbm, fac_hbm, half_hbm,
                  jump0, prod, half, pay,
                  res, dbuf, lbuf, corner, jumpv, prodv, halfv, block, sem):
    copies = Copies(sem)
    edges = (chip, far, near, other)
    dirs = [copies.fetch(dir_hbm.at[s, 0], dbuf.at[s]) for s in range(2)]
    facs = [fetch_lower(copies, fac_hbm.at[s, 0], lbuf.at[s]) for s in range(2)]
    corner_in = copies.fetch(half_hbm.at[:, pl.ds(K, CORN), :], corner)
    res_in = copies.fetch(res_hbm, res)
    jumped = jumps(sizes, sol_own, sol_other, inter, gram, edges, edge_grams(*edges))
    for s in range(2):
        jumpv[s] = jumped[s]
        copies.send(jumpv.at[s], jump0.at[s])
    for s in range(2):
        dirs[s].wait()
        prodv[s] = active_mask(sizes[s]) * dot(dbuf[s], jumpv[s].astype(BF16))
        copies.send(prodv.at[s], prod.at[s])
    corner_in.wait()
    corners = []
    for s in range(2):
        turned = times_lower_turned(jnp.transpose(prodv[s]).astype(BF16), lbuf.at[s], facs[s]).astype(BF16)
        halfv[s] = turned
        copies.send(halfv.at[s], half.at[s])
        corners.append(corner_mask(sizes[s]) * dot_turned(corner[s], turned))
    res_in.wait()
    cross = sum(jnp.sum(res[s] * jumpv[s], axis=0, keepdims=True) for s in range(2))
    energy = sum(jnp.sum(jumpv[s] * jumpv[s], axis=0, keepdims=True) for s in range(2))
    rows = [jnp.zeros((1, K), F32)] * 2 + list(split3(cross)) + list(split3(energy))
    send_payload(copies, pay, block, corners, rows_of((16, K), rows))
    copies.finish()


def back_next_kernel(sizes, half_hbm, fac_hbm, inter, chip, far, near, other,
                     half, lbuf, interv, e0, e1, e2, e3, sem):
    copies = Copies(sem)
    facs, halves_in = [], []
    for s in range(2):
        halves_in.append(copies.fetch(half_hbm.at[s], half.at[s]))
        facs.append(fetch_lower(copies, fac_hbm.at[s, 0], lbuf.at[s]))
    for s in range(2):
        halves_in[s].wait()
        for load in facs[s]:
            load.wait()
        interv[s] = active_mask(sizes[s]) * jnp.transpose(times_lower(half.at[s], lbuf.at[s]))
        copies.send(interv.at[s], inter.at[s])
    send_edges(copies, (e0, e1, e2, e3), (chip, far, near, other), interv, None)
    copies.finish()


def third_kernel(sizes, sol_own, sol_other, stats, inter, gram, chip, far, near, other,
                 old_chip, old_far, old_near, old_other, res_hbm, jump_hbm,
                 res1, jump1, pay, res, jump0, sem):
    copies = Copies(sem)
    edges = (chip, far, near, other)
    late = [copies.fetch(res_hbm, res), copies.fetch(jump_hbm, jump0)]
    grams = edge_grams(old_chip, old_far, old_near, old_other)
    again = jumps(sizes, sol_own, sol_other, inter, gram, edges, grams)
    for load in late:
        load.wait()
    step = stats[0:1] / (stats[1:2] + 1e-06)
    cross = jnp.zeros((1, K), F32)
    energy = jnp.zeros((1, K), F32)
    for s in range(2):
        before = res[s] - step * jump0[s]
        jumped = jump0[s] - step * again[s]
        res1[s] = before
        jump1[s] = jumped
        cross += jnp.sum(before * jumped, axis=0, keepdims=True)
        energy += jnp.sum(jumped * jumped, axis=0, keepdims=True)
    block = rows_of((8, K), [cross, energy])
    for dest in range(CS * YS):
        pay[dest] = block


def partial_kernel(rec, pay):
    total = sum(rec[b] for b in range(CS * YS))
    for dest in range(ZS * XS):
        pay[dest] = total


def last_kernel(rec, stats, res1, jump1, search, prod, mult, res, multv, resv, sem):
    copies = Copies(sem)
    total = sum(rec[b] for b in range(ZS * XS))
    first = stats[0:1] / (stats[1:2] + 1e-06)
    step = total[0:1] / (total[1:2] + 1e-06)
    for s in range(2):
        multv[s] = first * search[s] + step * (search[s] - first * prod[s])
        copies.send(multv.at[s], mult.at[s])
        resv[s] = res1[s] - step * jump1[s]
        copies.send(resv.at[s], res.at[s])
    copies.finish()


def all_to_all(value, axes):
    return lax.all_to_all(value, axes, split_axis=0, concat_axis=0)


def swap(value):
    return lax.ppermute(value, "core", [(0, 1), (1, 0)])


def exchange(chip, far, near, other):
    even = [(i, i ^ 1) for i in range(16)]
    odd = [(i, i + 1) for i in range(1, 15, 2)] + [(i + 1, i) for i in range(1, 15, 2)]
    rows, cols = ("z", "core"), ("x", "y")
    return (
        lax.ppermute(chip, rows, even),
        lax.ppermute(far, rows, odd),
        lax.ppermute(near, cols, even),
        lax.ppermute(other, cols, odd),
    )


def coarse_solution(own, snd, arrived, needed):
    pay3 = ((ZS, HALF + 16, K), BF16)
    rcv = swap(snd)
    (pay,) = call(pair_sum_kernel, [pay3], [VM] * 2, [HB], [(pay3[0][1:], BF16), sems(ZS)])(own, rcv)
    rec = all_to_all(pay, "z")
    pay, stats = call(
        z_sum_kernel,
        [((SY, HALF, K), BF16), ((8, K), F32)],
        [VM, AN, AN],
        [HB, VM],
        [((HALF, K), BF16), sems(SY)],
    )(rec, *arrived[2:])
    sol = all_to_all(pay, ("x", "y"))
    (sol,) = call(tie_kernel, [((SY, HALF, K), BF16)], [AN] * 3, [AN], aliases={0: 0})(sol, *arrived[:2])
    kinds = [(a.shape, a.dtype) for a in needed]
    needed = call(preload_kernel, kinds, [AN] + [HB] * len(kinds), [VM] * len(kinds), [sems(len(kinds))])(sol, *needed)
    sol = sol.reshape(SY * HALF, K)
    return sol, swap(sol), stats, needed


def local(factor, pre, coarse_inv, sizes, cmap, snow_level, pressure):
    sizes = sizes.reshape(2)
    whole = ((2, B, K), F32)
    gramed = ((2, B, K), BF16)
    halved = ((2, K, B), BF16)
    cornered = ((2, K + CORN, B), BF16)
    square = ((2, B, B), BF16)
    payload = ((SY, ROWS, K), BF16)
    block = (payload[0][1:], BF16)
    sent = [((HALF + 8, K), F32)] * 2

    def edges_of(width):
        return [((E, width), BF16)] * 2 + [((2, E, width), BF16)] * 2

    res, search, half, pay = call(
        first_kernel,
        [whole, whole, cornered, payload],
        [HB] * 6,
        [HB] * 4,
        [square, square, ((2, 1, B, K), BF16), whole, whole, cornered, block]
        + [((2, 1, B), jnp.int32), ((2, 1, CORN), jnp.int32), pltpu.SMEM((2,), jnp.int32), sems(20 + SY)],
    )(sizes, snow_level, cmap, pressure, pre, factor)
    rec = all_to_all(pay, ("x", "y"))
    wide = edges_of(2 * K)
    inter, gram, *edges = call(
        back_first_kernel,
        [whole, gramed] + wide,
        [SM, VM, HB, HB],
        [HB] * 6,
        [cornered, square, whole, gramed] + wide + [sems(18)],
    )(sizes, cmap, half, factor)
    arrived = exchange(*edges)
    own, snd, picked_inv = call(
        coarse_first_kernel,
        sent + [((E, B), BF16)],
        [VM, HB, HB],
        [VM, VM, HB],
        [((E, NC), BF16), ((E, B), BF16), ((NC, B), BF16), sems(2)],
    )(rec, coarse_inv, gram)
    sol_own, sol_other, _, needed = coarse_solution(own, snd, arrived, [inter, gram])
    jump0, prod, half1, pay = call(
        second_kernel,
        [whole, whole, halved, payload],
        [SM] + [VM] * 8 + [HB] * 4,
        [HB] * 4,
        [whole, square, square, ((2, CORN, B), BF16), whole, whole, halved, block, sems(24 + SY)],
    )(sizes, sol_own, sol_other, *needed, *arrived, res, pre, factor, half)
    rec = all_to_all(pay, ("x", "y"))
    slim = edges_of(K)
    inter1, *edges = call(
        back_next_kernel,
        [whole] + slim,
        [SM] + [HB] * 2,
        [HB] * 5,
        [halved, square, whole] + slim + [sems(16)],
    )(sizes, half1, factor)
    arrived1 = exchange(*edges)
    own, snd = call(coarse_next_kernel, sent, [VM] * 2 + [HB], [VM] * 2)(rec, picked_inv, inter1)
    sol_own, sol_other, stats, needed = coarse_solution(own, snd, arrived1, [inter1, gram, *arrived])
    res1, jump1, pay = call(
        third_kernel,
        [whole] * 2 + [((CS * YS, 8, K), F32)],
        [SM] + [VM] * 13 + [HB] * 2,
        [VM] * 3,
        [whole, whole, sems(2)],
    )(sizes, sol_own, sol_other, stats, *needed[:2], *arrived1, *needed[2:], res, jump0)
    rec = all_to_all(pay, ("core", "y"))
    (pay,) = call(partial_kernel, [((ZS * XS, 8, K), F32)], [VM], [VM])(rec)
    rec = all_to_all(pay, ("z", "x"))
    mult, res = call(last_kernel, [whole] * 2, [VM] * 6, [HB] * 2, [whole, whole, sems(4)])(
        rec, stats, res1, jump1, search, prod
    )
    return mult.reshape(2, 1, B, K), res.reshape(2, 1, B, K)


def solution(mesh):
    fine = Mesh(mesh.devices.reshape(ZS, CS, XS, YS), ("z", "core", "x", "y"))
    rows, cols = ("z", "core"), ("x", "y")
    return jax.shard_map(
        local,
        mesh=fine,
        in_specs=(
            P(rows, cols, None, None),
            P(rows, cols, None, None),
            P(cols, None),
            P(rows, cols),
            P(rows, cols, None),
            P(rows, cols, None),
            P(rows, cols, None, None),
        ),
        out_specs=(P(rows, cols, None, None), P(rows, cols, None, None)),
        check_vma=False,
    )
```

```python
import jax
import jax.numpy as jnp
from jax import lax
from jax.experimental import pallas as pl
from jax.experimental.pallas import tpu as pltpu
from jax.sharding import Mesh
from jax.sharding import PartitionSpec as P

B = 1024
E = 256
K = 128
CORN = 32
NC = 4096
GR = 32
GC = 16
ZS = 8
CS = 2
XS = 4
YS = 4
SY = XS * YS
STRIDE = B // CORN
ROWS = 80
HALF = 128
F32 = jnp.float32
BF16 = jnp.bfloat16
VMEM_LIMIT = 40 * 1024 * 1024

VM = pl.BlockSpec(memory_space=pltpu.VMEM)
SM = pl.BlockSpec(memory_space=pltpu.SMEM)
HB = pl.BlockSpec(memory_space=pltpu.HBM)
AN = pl.BlockSpec(memory_space=pl.ANY)


def dot(a, b):
    return jnp.dot(a, b, preferred_element_type=F32)


def iota(shape, dim):
    return lax.broadcasted_iota(jnp.int32, shape, dim)


def call(kernel, outs, in_specs, out_specs, scratch=(), aliases=None):
    run = pl.pallas_call(
        kernel,
        out_shape=[
            pltpu.HBM(shape, dtype) if spec is HB else jax.ShapeDtypeStruct(shape, dtype)
            for (shape, dtype), spec in zip(outs, out_specs)
        ],
        in_specs=in_specs,
        out_specs=out_specs,
        scratch_shapes=[pltpu.VMEM(*item) if isinstance(item, tuple) else item for item in scratch],
        input_output_aliases=aliases or {},
        compiler_params=pltpu.CompilerParams(vmem_limit_bytes=VMEM_LIMIT),
    )

    def placed(*args):
        return run(
            *[pltpu.with_memory_space_constraint(a, pltpu.HBM) if spec is HB else a for a, spec in zip(args, in_specs)]
        )

    return placed


class Copies:
    def __init__(self, sems):
        self.sems = sems
        self.count = 0
        self.out = []

    def fetch(self, source, target):
        copy = pltpu.make_async_copy(source, target, self.sems.at[self.count])
        self.count += 1
        copy.start()
        return copy

    def send(self, source, target):
        self.out.append(self.fetch(source, target))

    def finish(self):
        for copy in self.out:
            copy.wait()


def sems(count):
    return pltpu.SemaphoreType.DMA((count,))


def fetch_lower(copies, source, target):
    loads = []
    for block in range(B // E):
        rows, cols = pl.ds(block * E, E), pl.ds(0, (block + 1) * E)
        loads.append(copies.fetch(source.at[rows, cols], target.at[rows, cols]))
    return loads


def dot_turned(a, b):
    return lax.dot_general(a, b, (((1,), (1,)), ((), ())), preferred_element_type=F32)


def times_lower_turned(left, matrix, loads):
    for load in loads:
        load.wait()
    parts = []
    for block in range(B // E):
        width = (block + 1) * E
        parts.append(dot_turned(left[:, :width], matrix[block * E : width, :width]))
    return jnp.concatenate(parts, axis=1)


def times_lower(left, matrix):
    parts = []
    for block in range(B // E):
        start = block * E
        parts.append(dot(left[:, start:], matrix[start:, start : start + E]))
    return jnp.concatenate(parts, axis=1)


def split2(value):
    high = value.astype(BF16)
    low = (value - high.astype(F32)).astype(BF16)
    return high, low


def split3(value):
    high, _ = split2(value)
    rest = value - high.astype(F32)
    mid, low = split2(rest)
    return high, mid, low


def active_mask(size):
    return ((iota((B, K), 0) & (E - 1)) < size).astype(F32)


def rows_of(shape, rows):
    index = iota(shape, 0)
    result = jnp.zeros(shape, F32)
    for number, row in enumerate(rows):
        result = jnp.where(index == number, jnp.broadcast_to(row.astype(F32), shape), result)
    return result


def send_payload(copies, pay, block, corners, tail):
    block[...] = jnp.concatenate([c.astype(BF16) for c in corners] + [tail.astype(BF16)], axis=0)
    for dest in range(SY):
        copies.send(block, pay.at[dest])


def send_edges(copies, bufs, targets, interface, extra):
    chip, far, near, other = bufs
    core = lax.axis_index("core")
    odd = lax.axis_index("y") & 1

    def packed(s, edge):
        rows = pl.ds(pl.multiple_of(edge * E, E), E)
        parts = [interface[s, rows, :].astype(BF16)]
        if extra is not None:
            parts.append(extra[s, rows, :])
        return jnp.concatenate(parts, axis=1)

    chip[...] = packed(1 - core, 1 - core)
    far[...] = packed(core, core)
    for s in range(2):
        near[s] = packed(s, 3 - odd)
        other[s] = packed(s, 2 + odd)
    for source, target in zip(bufs, targets):
        copies.send(source, target)


def first_kernel(sizes_hbm, snow_hbm, cmap_hbm, press_hbm, dir_hbm, fac_hbm,
                 res, search, half, pay, dbuf, lbuf, press, resv, searchv, halfv, block, snow, cmap, sizes, sem):
    copies = Copies(sem)
    small = [copies.fetch(a, b) for a, b in ((sizes_hbm, sizes), (snow_hbm, snow), (cmap_hbm, cmap))]
    load = copies.fetch(press_hbm, press)
    dirs, facs = [], []
    for s in range(2):
        dirs.append(copies.fetch(dir_hbm.at[s, 0], dbuf.at[s]))
    for s in range(2):
        facs.append(fetch_lower(copies, fac_hbm.at[s, 0], lbuf.at[s]))
    grid_row = lax.axis_index("z") * (2 * CS) + lax.axis_index("core") * 2
    grid_col = lax.axis_index("x") * YS + lax.axis_index("y")
    for copy in small:
        copy.wait()
    masks = [active_mask(sizes[s]) for s in range(2)]
    pick = jnp.where(iota((CORN, B), 1) == iota((CORN, B), 0) * STRIDE, 1.0, 0.0).astype(BF16)
    columns = []
    for s in range(2):
        place = jnp.full((1, B), grid_row + s + grid_col, jnp.int32).astype(F32)
        drift = 1.0 + 2.0 * place / (GR + GC - 2)
        depth = 0.5 + 0.25 * snow[s].astype(F32)
        present = (iota((1, B), 1) & (E - 1)) < sizes[s]
        scale = jnp.where(present, depth * drift, 0.0)
        columns.append(jnp.transpose(jnp.broadcast_to(scale, (K, B))))
    load.wait()
    for s in range(2):
        resv[s] = press[s, 0].astype(F32) * columns[s]
        copies.send(resv.at[s], res.at[s])
    for s in range(2):
        dirs[s].wait()
        searchv[s] = masks[s] * dot(dbuf[s], resv[s].astype(BF16))
        copies.send(searchv.at[s], search.at[s])
    corners = []
    for s in range(2):
        left = jnp.concatenate([jnp.transpose(searchv[s]).astype(BF16), pick], axis=0)
        turned = times_lower_turned(left, lbuf.at[s], facs[s]).astype(BF16)
        halfv[s] = turned
        copies.send(halfv.at[s], half.at[s])
        rows = dot_turned(turned[K:], turned[:K])
        corners.append(corner_mask(sizes[s]) * rows)
    cm = two_rows(cmap)
    tail = rows_of((16, K), [(cm >> 8).astype(F32), (cm & 255).astype(F32)])
    send_payload(copies, pay, block, corners, tail)
    copies.finish()


def corner_mask(size):
    return (((iota((CORN, K), 0) * STRIDE) & (E - 1)) < size).astype(F32)


def tiled_row(row):
    return jnp.concatenate([row] * (K // CORN), axis=1)


def two_rows(cmap):
    lane = iota((1, K), 1)
    return jnp.where((lane & CORN) == 0, tiled_row(cmap[0]), tiled_row(cmap[1]))


def back_first_kernel(sizes, cmap, half_hbm, fac_hbm, inter, gram, chip, far, near, other,
                      half, lbuf, interv, gramv, e0, e1, e2, e3, sem):
    copies = Copies(sem)
    facs, halves_in = [], []
    for s in range(2):
        halves_in.append(copies.fetch(half_hbm.at[s], half.at[s]))
        facs.append(fetch_lower(copies, fac_hbm.at[s, 0], lbuf.at[s]))
    lane = iota((B, K), 1)
    for s in range(2):
        mask = active_mask(sizes[s])
        square = jnp.transpose(jnp.broadcast_to(tiled_row(cmap[s]), (K, K)))
        column = jnp.concatenate([square] * (B // K), axis=0)
        digits = jnp.where(lane < 96, column >> 8, column & 255).astype(F32)
        halves_in[s].wait()
        for load in facs[s]:
            load.wait()
        back = jnp.transpose(times_lower(half.at[s], lbuf.at[s]))
        interv[s] = mask * back[:, :K]
        copies.send(interv.at[s], inter.at[s])
        ghigh, glow = split2(mask * jnp.concatenate([back[:, K:], jnp.zeros((B, K - CORN), F32)], axis=1))
        low_moved = pltpu.roll(glow.astype(F32), CORN, axis=1)
        gramv[s] = jnp.where(
            lane < CORN, ghigh.astype(F32), jnp.where(lane < 2 * CORN, low_moved, digits)
        ).astype(BF16)
        copies.send(gramv.at[s], gram.at[s])
    send_edges(copies, (e0, e1, e2, e3), (chip, far, near, other), interv, gramv)
    copies.finish()


def coarse_rows(rec):
    return jnp.concatenate([rec[b, 0:64, :] for b in range(SY)], axis=0)


def halves(value, stats, own, snd):
    mine = lax.axis_index("core") == 0
    tail = rows_of((8, K), stats)
    own[0:HALF] = jnp.where(mine, value[:HALF], value[HALF:])
    snd[0:HALF] = jnp.where(mine, value[HALF:], value[:HALF])
    own[HALF : HALF + 8] = tail
    snd[HALF : HALF + 8] = tail


def coarse_first_kernel(rec, coarse_hbm, _, own, snd, picked_inv, coarse, matrix, hot, sem):
    copies = Copies(sem)
    load = copies.fetch(coarse_hbm, coarse)
    lane = iota((1, K), 1)
    tails = [rec[b, 64:80, :].astype(F32) for b in range(SY)]

    def row(number):
        parts = [
            jnp.where(lane < 64, tails[2 * m][number : number + 1], tails[2 * m + 1][number : number + 1])
            for m in range(SY // 2)
        ]
        return jnp.concatenate(parts, axis=1)

    high, low = row(0), row(1)
    low_hot = jnp.where(iota((E, B), 0) == low.astype(jnp.int32), 1.0, 0.0).astype(BF16)
    high_hot = jnp.where(iota((NC // E, B), 0) == high.astype(jnp.int32), 1.0, 0.0).astype(BF16)
    for digit in range(NC // E):
        hot[digit * E : (digit + 1) * E] = low_hot * high_hot[digit : digit + 1]
    load.wait()
    matrix[...] = dot(coarse[...], hot[...]).astype(BF16)
    copies.send(matrix, picked_inv)
    halves(dot(matrix[...], coarse_rows(rec)), [], own, snd)
    copies.finish()


def coarse_next_kernel(rec, picked_inv, _, own, snd):
    value = dot(picked_inv[...], coarse_rows(rec))
    tails = sum(rec[b, 64:80, :].astype(F32) for b in range(SY))
    stats = [tails[q : q + 1] + tails[q + 1 : q + 2] + tails[q + 2 : q + 3] for q in (2, 5)]
    halves(value, stats, own, snd)


def pair_sum_kernel(own, rcv, pay, block, sem):
    copies = Copies(sem)
    total = own[...] + rcv[...]
    rows = []
    for q in range(2):
        rows += list(split3(total[HALF + q : HALF + q + 1]))
    tail = rows_of((16, K), rows).astype(BF16)
    block[...] = jnp.concatenate([total[:HALF].astype(BF16), tail], axis=0)
    for dest in range(ZS):
        copies.send(block, pay.at[dest])
    copies.finish()


def z_sum_kernel(rec, _, __, pay, stats, block, sem):
    copies = Copies(sem)
    total = sum(rec[z].astype(F32) for z in range(ZS))
    block[...] = total[:HALF].astype(BF16)
    for dest in range(SY):
        copies.send(block, pay.at[dest])
    rows = total[HALF:]
    stats[...] = rows_of(
        (8, K), [rows[q : q + 1] + rows[q + 1 : q + 2] + rows[q + 2 : q + 3] for q in (0, 3)]
    )
    copies.finish()


def preload_kernel(_, *refs):
    count = len(refs) // 2
    copies = Copies(refs[-1])
    for source, target in zip(refs[:count], refs[count:-1]):
        copies.send(source, target)
    copies.finish()


def tie_kernel(source, _, __, target):
    pass


def jumps(sizes, sol_own, sol_other, inter, gram, edges, grams):
    core = lax.axis_index("core")
    odd = lax.axis_index("y") & 1
    chip, far, near, other = edges
    gchip, gfar, gnear, gother = grams

    def ordered(flag, a, b):
        return jnp.where(flag == 0, b, a), jnp.where(flag == 0, a, b)

    north, south = ordered(core, chip[...], far[...])
    gnorth, gsouth = ordered(core, gchip, gfar)
    west, east = ordered(odd, near[...], other[...])
    gwest, geast = ordered(odd, gnear, gother)
    gram_edges = [gram[0, 0:CORN, :], gram[1, 0:CORN, :], gnorth[0:CORN], gsouth[0:CORN]]
    gram_edges += [g[s, 0:CORN, :] for g in (gwest, geast) for s in range(2)]
    digits = jnp.concatenate(gram_edges, axis=0).astype(F32)
    cm = digits[:, 64:65].astype(jnp.int32) * 256 + digits[:, 96:97].astype(jnp.int32)
    half = ((cm >> 7) & 1) ^ core
    place = half * 2048 + (cm >> 8) * HALF + (cm & (HALF - 1))
    hot = jnp.where(iota((8 * CORN, NC), 1) == place, 1.0, 0.0).astype(BF16)
    picks = (dot(hot[:, :2048], sol_own[...]) + dot(hot[:, 2048:], sol_other[...])).astype(BF16)
    zero = jnp.zeros((2 * CORN, K), BF16)

    def stacked(number):
        rows = picks[number * CORN : (number + 1) * CORN]
        return jnp.concatenate([rows, rows, zero], axis=0)

    full = [inter[s] + dot(gram[s], stacked(s)) for s in range(2)]

    def arrived(edge, gedge, number):
        return edge[:, :K].astype(F32) + dot(gedge, stacked(number))

    above = [arrived(north, gnorth, 2), full[0][E : 2 * E]]
    below = [full[1][0:E], arrived(south, gsouth, 3)]
    left = [arrived(west[s], gwest[s], 4 + s) for s in range(2)]
    right = [arrived(east[s], geast[s], 6 + s) for s in range(2)]
    return [
        active_mask(sizes[s]) * (full[s] - jnp.concatenate([above[s], below[s], left[s], right[s]], axis=0))
        for s in range(2)
    ]


def edge_grams(chip, far, near, other):
    return chip[:, K:], far[:, K:], near[:, :, K:], other[:, :, K:]


def second_kernel(sizes, sol_own, sol_other, inter, gram, chip, far, near, other,
                  res_hbm, dir_hbm, fac_hbm, half_hbm,
                  jump0, prod, half, pay,
                  res, dbuf, lbuf, corner, jumpv, prodv, halfv, block, sem):
    copies = Copies(sem)
    edges = (chip, far, near, other)
    dirs = [copies.fetch(dir_hbm.at[s, 0], dbuf.at[s]) for s in range(2)]
    facs = [fetch_lower(copies, fac_hbm.at[s, 0], lbuf.at[s]) for s in range(2)]
    corner_in = copies.fetch(half_hbm.at[:, pl.ds(K, CORN), :], corner)
    res_in = copies.fetch(res_hbm, res)
    jumped = jumps(sizes, sol_own, sol_other, inter, gram, edges, edge_grams(*edges))
    for s in range(2):
        jumpv[s] = jumped[s]
        copies.send(jumpv.at[s], jump0.at[s])
    for s in range(2):
        dirs[s].wait()
        prodv[s] = active_mask(sizes[s]) * dot(dbuf[s], jumpv[s].astype(BF16))
        copies.send(prodv.at[s], prod.at[s])
    corner_in.wait()
    corners = []
    for s in range(2):
        turned = times_lower_turned(jnp.transpose(prodv[s]).astype(BF16), lbuf.at[s], facs[s]).astype(BF16)
        halfv[s] = turned
        copies.send(halfv.at[s], half.at[s])
        corners.append(corner_mask(sizes[s]) * dot_turned(corner[s], turned))
    res_in.wait()
    cross = sum(jnp.sum(res[s] * jumpv[s], axis=0, keepdims=True) for s in range(2))
    energy = sum(jnp.sum(jumpv[s] * jumpv[s], axis=0, keepdims=True) for s in range(2))
    rows = [jnp.zeros((1, K), F32)] * 2 + list(split3(cross)) + list(split3(energy))
    send_payload(copies, pay, block, corners, rows_of((16, K), rows))
    copies.finish()


def back_next_kernel(sizes, half_hbm, fac_hbm, inter, chip, far, near, other,
                     half, lbuf, interv, e0, e1, e2, e3, sem):
    copies = Copies(sem)
    facs, halves_in = [], []
    for s in range(2):
        halves_in.append(copies.fetch(half_hbm.at[s], half.at[s]))
        facs.append(fetch_lower(copies, fac_hbm.at[s, 0], lbuf.at[s]))
    for s in range(2):
        halves_in[s].wait()
        for load in facs[s]:
            load.wait()
        interv[s] = active_mask(sizes[s]) * jnp.transpose(times_lower(half.at[s], lbuf.at[s]))
        copies.send(interv.at[s], inter.at[s])
    send_edges(copies, (e0, e1, e2, e3), (chip, far, near, other), interv, None)
    copies.finish()


def third_kernel(sizes, sol_own, sol_other, stats, inter, gram, chip, far, near, other,
                 old_chip, old_far, old_near, old_other, res_hbm, jump_hbm,
                 res1, jump1, pay, res, jump0, sem):
    copies = Copies(sem)
    edges = (chip, far, near, other)
    late = [copies.fetch(res_hbm, res), copies.fetch(jump_hbm, jump0)]
    grams = edge_grams(old_chip, old_far, old_near, old_other)
    again = jumps(sizes, sol_own, sol_other, inter, gram, edges, grams)
    for load in late:
        load.wait()
    step = stats[0:1] / (stats[1:2] + 1e-06)
    cross = jnp.zeros((1, K), F32)
    energy = jnp.zeros((1, K), F32)
    for s in range(2):
        before = res[s] - step * jump0[s]
        jumped = jump0[s] - step * again[s]
        res1[s] = before
        jump1[s] = jumped
        cross += jnp.sum(before * jumped, axis=0, keepdims=True)
        energy += jnp.sum(jumped * jumped, axis=0, keepdims=True)
    block = rows_of((8, K), [cross, energy])
    for dest in range(CS * SY):
        pay[dest] = block


def partial_kernel(rec, pay):
    total = sum(rec[b] for b in range(CS * SY))
    for dest in range(ZS):
        pay[dest] = total


def last_kernel(rec, stats, res1, jump1, search, prod, mult, res, multv, resv, sem):
    copies = Copies(sem)
    total = sum(rec[b] for b in range(ZS))
    first = stats[0:1] / (stats[1:2] + 1e-06)
    step = total[0:1] / (total[1:2] + 1e-06)
    for s in range(2):
        multv[s] = first * search[s] + step * (search[s] - first * prod[s])
        copies.send(multv.at[s], mult.at[s])
        resv[s] = res1[s] - step * jump1[s]
        copies.send(resv.at[s], res.at[s])
    copies.finish()


def all_to_all(value, axes):
    return lax.all_to_all(value, axes, split_axis=0, concat_axis=0)


def swap(value):
    return lax.ppermute(value, "core", [(0, 1), (1, 0)])


def exchange(chip, far, near, other):
    even = [(i, i ^ 1) for i in range(16)]
    odd = [(i, i + 1) for i in range(1, 15, 2)] + [(i + 1, i) for i in range(1, 15, 2)]
    rows, cols = ("z", "core"), ("x", "y")
    return (
        lax.ppermute(chip, rows, even),
        lax.ppermute(far, rows, odd),
        lax.ppermute(near, cols, even),
        lax.ppermute(other, cols, odd),
    )


def coarse_solution(own, snd, arrived, needed):
    pay3 = ((ZS, HALF + 16, K), BF16)
    rcv = swap(snd)
    (pay,) = call(pair_sum_kernel, [pay3], [VM] * 2, [HB], [(pay3[0][1:], BF16), sems(ZS)])(own, rcv)
    rec = all_to_all(pay, "z")
    pay, stats = call(
        z_sum_kernel,
        [((SY, HALF, K), BF16), ((8, K), F32)],
        [VM, AN, AN],
        [HB, VM],
        [((HALF, K), BF16), sems(SY)],
    )(rec, *arrived[2:])
    sol = all_to_all(pay, ("x", "y"))
    (sol,) = call(tie_kernel, [((SY, HALF, K), BF16)], [AN] * 3, [AN], aliases={0: 0})(sol, *arrived[:2])
    kinds = [(a.shape, a.dtype) for a in needed]
    needed = call(preload_kernel, kinds, [AN] + [HB] * len(kinds), [VM] * len(kinds), [sems(len(kinds))])(sol, *needed)
    sol = sol.reshape(SY * HALF, K)
    return sol, swap(sol), stats, needed


def local(factor, pre, coarse_inv, sizes, cmap, snow_level, pressure):
    sizes = sizes.reshape(2)
    whole = ((2, B, K), F32)
    gramed = ((2, B, K), BF16)
    halved = ((2, K, B), BF16)
    cornered = ((2, K + CORN, B), BF16)
    square = ((2, B, B), BF16)
    payload = ((SY, ROWS, K), BF16)
    block = (payload[0][1:], BF16)
    sent = [((HALF + 8, K), F32)] * 2

    def edges_of(width):
        return [((E, width), BF16)] * 2 + [((2, E, width), BF16)] * 2

    res, search, half, pay = call(
        first_kernel,
        [whole, whole, cornered, payload],
        [HB] * 6,
        [HB] * 4,
        [square, square, ((2, 1, B, K), BF16), whole, whole, cornered, block]
        + [((2, 1, B), jnp.int32), ((2, 1, CORN), jnp.int32), pltpu.SMEM((2,), jnp.int32), sems(20 + SY)],
    )(sizes, snow_level, cmap, pressure, pre, factor)
    rec = all_to_all(pay, ("x", "y"))
    wide = edges_of(2 * K)
    inter, gram, *edges = call(
        back_first_kernel,
        [whole, gramed] + wide,
        [SM, VM, HB, HB],
        [HB] * 6,
        [cornered, square, whole, gramed] + wide + [sems(18)],
    )(sizes, cmap, half, factor)
    arrived = exchange(*edges)
    own, snd, picked_inv = call(
        coarse_first_kernel,
        sent + [((E, B), BF16)],
        [VM, HB, HB],
        [VM, VM, HB],
        [((E, NC), BF16), ((E, B), BF16), ((NC, B), BF16), sems(2)],
    )(rec, coarse_inv, gram)
    sol_own, sol_other, _, needed = coarse_solution(own, snd, arrived, [inter, gram])
    jump0, prod, half1, pay = call(
        second_kernel,
        [whole, whole, halved, payload],
        [SM] + [VM] * 8 + [HB] * 4,
        [HB] * 4,
        [whole, square, square, ((2, CORN, B), BF16), whole, whole, halved, block, sems(24 + SY)],
    )(sizes, sol_own, sol_other, *needed, *arrived, res, pre, factor, half)
    rec = all_to_all(pay, ("x", "y"))
    slim = edges_of(K)
    inter1, *edges = call(
        back_next_kernel,
        [whole] + slim,
        [SM] + [HB] * 2,
        [HB] * 5,
        [halved, square, whole] + slim + [sems(16)],
    )(sizes, half1, factor)
    arrived1 = exchange(*edges)
    own, snd = call(coarse_next_kernel, sent, [VM] * 2 + [HB], [VM] * 2)(rec, picked_inv, inter1)
    sol_own, sol_other, stats, needed = coarse_solution(own, snd, arrived1, [inter1, gram, *arrived])
    res1, jump1, pay = call(
        third_kernel,
        [whole] * 2 + [((CS * SY, 8, K), F32)],
        [SM] + [VM] * 13 + [HB] * 2,
        [VM] * 3,
        [whole, whole, sems(2)],
    )(sizes, sol_own, sol_other, stats, *needed[:2], *arrived1, *needed[2:], res, jump0)
    rec = all_to_all(pay, ("core", "x", "y"))
    (pay,) = call(partial_kernel, [((ZS, 8, K), F32)], [VM], [VM])(rec)
    rec = all_to_all(pay, "z")
    mult, res = call(last_kernel, [whole] * 2, [VM] * 6, [HB] * 2, [whole, whole, sems(4)])(
        rec, stats, res1, jump1, search, prod
    )
    return mult.reshape(2, 1, B, K), res.reshape(2, 1, B, K)


def solution(mesh):
    fine = Mesh(mesh.devices.reshape(ZS, CS, XS, YS), ("z", "core", "x", "y"))
    rows, cols = ("z", "core"), ("x", "y")
    return jax.shard_map(
        local,
        mesh=fine,
        in_specs=(
            P(rows, cols, None, None),
            P(rows, cols, None, None),
            P(cols, None),
            P(rows, cols),
            P(rows, cols, None),
            P(rows, cols, None),
            P(rows, cols, None, None),
        ),
        out_specs=(P(rows, cols, None, None), P(rows, cols, None, None)),
        check_vma=False,
    )
```
